32 devices in a mesh: ctx: 16 (over z, y, core), grp: 2 (over x).
Axes of the slice: x: 2, y: 2, z: 4, core: 2. Of those that a mesh axis runs over, the one named last changes fastest.
Arguments:
- queries: bfloat16 [8192, 1024], P('ctx', 'grp'), may hold values from -6 to 6
- key_rows: bfloat16 [8192, 256], P('ctx', 'grp'), may hold values from -6 to 6
- value_rows: bfloat16 [8192, 256], P('ctx', 'grp'), may hold values from -6 to 6
- output_rows: bfloat16 [8192, 1024], P('ctx', 'grp'), may hold values from -6 to 6
- output_grad: bfloat16 [8192, 1024], P('ctx', 'grp'), may hold values from -6 to 6
- log_normalizer: float32 [8192, 8], P('ctx', 'grp'), may hold values from 4 to 6
- selection: int32 [16, 3], replicated, may hold values from 0 to 14, as said below
- query_weight: bfloat16 [4096, 1024], P(None, 'grp'), may hold values from -0.09375 to 0.09375
- key_weight: bfloat16 [4096, 256], P(None, 'grp'), may hold values from -0.09375 to 0.09375
- value_weight: bfloat16 [4096, 256], P(None, 'grp'), may hold values from -0.09375 to 0.09375
Outputs:
- input_grad: bfloat16 [8192, 4096], P('ctx', 'grp')
The draws below stay inside these ranges and needn't reach their ends.
Inputs may be any that keep to these rules, and one draw needn't show every extreme that they name: `selection`: row b names the 3 blocks chosen for query block b: distinct blocks below b, among them always block b - 1; a row with fewer than 3 blocks below it names all of them and repeats b itself in the remaining places.
All inputs are finite; a program needn't handle non-finite values.
Results may differ from the reference program's by a relative error of at most 0.019.
Values may be sent and summed in bfloat16 or wider, within the bound.
A program may use at most 128 MiB of HBM per device.

```python
import jax
import jax.numpy as jnp
from jax import lax

D = 4096
HD = 128
QPK = 4
KV_DEV = 1
BLOCK = 512
TOPK = 3
KV_HEADS = 2
HEADS = 8
HF = 1024
KF = 256
SEQ = 8192
NB = 16
N_GRP = 2


def draw_selection(key, part):
    key = jax.random.fold_in(key, 7)
    block_ids = jnp.arange(NB, dtype=jnp.int32)
    ranks = jax.random.randint(key, (NB, NB), 0, 1 << 20, dtype=jnp.int32) * NB + block_ids[None, :]
    ranks = jnp.where(block_ids[None, :] == block_ids[:, None] - 1, 1 << 30, ranks)
    ranks = jnp.where(block_ids[None, :] < block_ids[:, None], ranks, -1)
    values, indices = lax.top_k(ranks, TOPK)
    return jnp.where(values >= 0, indices, block_ids[:, None]).astype(jnp.int32)


def block_levels(own_key, shape, pieces, low, top_value):
    gain, own = 1.0, jax.random.fold_in(own_key, 6)
    for dim, blocks in pieces:
        steps = jnp.exp(jax.random.uniform(jax.random.fold_in(own, dim), (blocks,), jnp.float32, low / len(pieces), top_value / len(pieces)))
        gain = gain * jnp.repeat(steps, shape[dim] // blocks).reshape([-1 if axis == dim else 1 for axis in range(len(shape))])
    return gain


def gaussian(stream_key, extent, width, reach, pieces=(), held_as=jnp.bfloat16):
    entries = jax.random.normal(stream_key, extent, jnp.float32) * width
    if len(pieces) > 0:
        entries = block_levels(stream_key, extent, pieces, -0.22, 0.18) * entries
    return jnp.clip(entries, min=-reach, max=reach).astype(held_as)


def setup_inputs(seed: int = 0) -> dict:
    keys = jax.random.split(jax.random.key(seed), 11)
    queries = gaussian(keys[0], (SEQ, HF), 1.0, 6.0, ((0, 16), (1, 2)))
    key_rows = gaussian(keys[1], (SEQ, KF), 1.0, 6.0, ((0, 16), (1, 2)))
    value_rows = gaussian(keys[2], (SEQ, KF), 1.0, 6.0, ((0, 16), (1, 2)))
    output_rows = gaussian(keys[3], (SEQ, HF), 1.0, 6.0, ((0, 16), (1, 2)))
    output_grad = gaussian(keys[4], (SEQ, HF), 1.0, 6.0, ((0, 16), (1, 2)))
    log_normalizer = jnp.clip(4.0 + 2.0 * jax.random.uniform(keys[5], (SEQ, HEADS), jnp.float32) ** block_levels(keys[5], (SEQ, HEADS), ((0, 16), (1, 2)), -0.2, 0.2), 4.0, 6.0)
    selection = draw_selection(jax.random.fold_in(keys[10], 71), 0)
    query_weight = gaussian(keys[7], (D, HF), D ** -0.5, 0.09375, ((1, 2),))
    key_weight = gaussian(keys[8], (D, KF), D ** -0.5, 0.09375, ((1, 2),))
    value_weight = gaussian(keys[9], (D, KF), D ** -0.5, 0.09375, ((1, 2),))
    return dict(queries=queries, key_rows=key_rows, value_rows=value_rows, output_rows=output_rows, output_grad=output_grad, log_normalizer=log_normalizer, selection=selection, query_weight=query_weight, key_weight=key_weight, value_weight=value_weight)


def reference(queries, key_rows, value_rows, output_rows, output_grad, log_normalizer, selection, query_weight, key_weight, value_weight):
    scaling = float(HD) ** -0.5
    query_full = queries.astype(jnp.float32).reshape(SEQ, KV_HEADS, QPK, HD)
    key_full = key_rows.astype(jnp.float32).reshape(SEQ, KV_HEADS, HD)
    value_full = value_rows.astype(jnp.float32).reshape(SEQ, KV_HEADS, HD)
    output_full = output_rows.astype(jnp.float32).reshape(SEQ, KV_HEADS, QPK, HD)
    cotangent = output_grad.astype(jnp.float32).reshape(SEQ, KV_HEADS, QPK, HD)
    row_delta = jnp.sum(output_full * cotangent, axis=-1)
    norm_full = log_normalizer.reshape(SEQ, KV_HEADS, QPK)
    offsets = jnp.arange(BLOCK, dtype=jnp.int32)
    causal = offsets[None, :] <= offsets[:, None]

    def block_step(totals, block_index):
        key_total, value_total = totals
        row_start = block_index * BLOCK
        query_block = lax.dynamic_slice_in_dim(query_full, row_start, BLOCK, 0)
        grad_block = lax.dynamic_slice_in_dim(cotangent, row_start, BLOCK, 0)
        norm_block = lax.dynamic_slice_in_dim(norm_full, row_start, BLOCK, 0).transpose(1, 2, 0)[:, :, :, None]
        delta_block = lax.dynamic_slice_in_dim(row_delta, row_start, BLOCK, 0).transpose(1, 2, 0)[:, :, :, None]
        chosen_row = lax.dynamic_index_in_dim(selection, block_index, 0, keepdims=False).astype(jnp.int32)
        visited = jnp.concatenate([jnp.reshape(block_index, (1,)).astype(jnp.int32), chosen_row])
        keys_seen = jnp.concatenate([lax.dynamic_slice_in_dim(key_full, visited[column] * BLOCK, BLOCK, 0) for column in range(TOPK + 1)], axis=0)
        values_seen = jnp.concatenate([lax.dynamic_slice_in_dim(value_full, visited[column] * BLOCK, BLOCK, 0) for column in range(TOPK + 1)], axis=0)
        allowed = jnp.concatenate([causal] + [jnp.broadcast_to(visited[column] < block_index, (BLOCK, BLOCK)) for column in range(1, TOPK + 1)], axis=1)
        scores = jnp.einsum("qgpd,kgd->gpqk", query_block, keys_seen) * scaling
        probs = jnp.where(allowed[None, None], jnp.exp(scores - norm_block), 0.0)
        prob_grad = jnp.einsum("qgpd,kgd->gpqk", grad_block, values_seen)
        score_grad = probs * (prob_grad - delta_block)
        probs_half = lax.optimization_barrier(probs.astype(jnp.bfloat16)).astype(jnp.float32)
        score_half = lax.optimization_barrier(score_grad.astype(jnp.bfloat16)).astype(jnp.float32)
        value_part = jnp.einsum("gpqk,qgpd->kgd", probs_half, grad_block)
        key_part = jnp.einsum("gpqk,qgpd->kgd", score_half, query_block)
        query_grad = (jnp.einsum("gpqk,kgd->qgpd", score_half, keys_seen) * scaling).astype(jnp.bfloat16)
        for column in range(TOPK + 1):
            target = visited[column] * BLOCK
            key_total = lax.dynamic_update_slice_in_dim(key_total, lax.dynamic_slice_in_dim(key_total, target, BLOCK, 0) + key_part[column * BLOCK:(column + 1) * BLOCK], target, 0)
            value_total = lax.dynamic_update_slice_in_dim(value_total, lax.dynamic_slice_in_dim(value_total, target, BLOCK, 0) + value_part[column * BLOCK:(column + 1) * BLOCK], target, 0)
        return (key_total, value_total), query_grad

    zeroed = jnp.zeros((SEQ, KV_HEADS, HD), jnp.float32)
    (key_total, value_total), query_blocks = lax.scan(block_step, (zeroed, zeroed), jnp.arange(NB, dtype=jnp.int32))
    grad_query = query_blocks.reshape(SEQ, HEADS * HD)
    grad_key = (key_total * scaling).astype(jnp.bfloat16).reshape(SEQ, KV_HEADS * HD)
    grad_value = value_total.astype(jnp.bfloat16).reshape(SEQ, KV_HEADS * HD)
    query_width = QPK * KV_DEV * HD
    key_width = KV_DEV * HD
    combined = jnp.zeros((SEQ, D), jnp.float32)
    for group in range(N_GRP):
        query_cols = slice(group * query_width, (group + 1) * query_width)
        key_cols = slice(group * key_width, (group + 1) * key_width)
        partial_sum = jnp.dot(grad_query[:, query_cols], query_weight[:, query_cols].T, preferred_element_type=jnp.float32)
        partial_sum = partial_sum + jnp.dot(grad_key[:, key_cols], key_weight[:, key_cols].T, preferred_element_type=jnp.float32)
        partial_sum = partial_sum + jnp.dot(grad_value[:, key_cols], value_weight[:, key_cols].T, preferred_element_type=jnp.float32)
        combined = combined + lax.optimization_barrier(partial_sum.astype(jnp.bfloat16)).astype(jnp.float32)
    return combined.astype(jnp.bfloat16)
```

```python
import functools
import math

import jax
import jax.numpy as jnp
from jax import lax
from jax.experimental import pallas as pl
from jax.experimental.pallas import tpu as pltpu
from jax.sharding import PartitionSpec as P

HD = 128
BLOCK = 512
TOPK = 3
MESH = pl.DeviceIdType.MESH
SCALE = float(HD) ** (-0.5)
LOG2E = math.log2(math.e)
VMEM_LIMIT = 56 * 1024 * 1024
NT = (((1,), (1,)), ((), ()))
NN = (((1,), (0,)), ((), ()))


def place():
    me = lax.axis_index("ctx")
    return me, me // 4, (me // 2) % 2, me % 2


def sibling_of(me, core):
    return me + 1 - 2 * core


def beside(me, column):
    return me + 2 - 4 * column


def remote(src, dst, send, recv, target):
    return pltpu.make_async_remote_copy(
        src_ref=src, dst_ref=dst, send_sem=send, recv_sem=recv,
        device_id={"ctx": target}, device_id_type=MESH,
    )


def greet(target):
    pl.semaphore_signal(
        pltpu.get_barrier_semaphore(), inc=1, device_id={"ctx": target}, device_id_type=MESH
    )


def gather_kernel(planes, kv_ref, all_ref, own_sem, z_send, z_recv, y_send, y_recv, c_send, c_recv):
    me, z, y, c = place()
    sibling, side = sibling_of(me, c), beside(me, y)
    greet(sibling)
    greet(side)

    @pl.when(z > 0)
    def _():
        greet(me - 4)

    own = pltpu.make_async_copy(kv_ref, all_ref.at[z, c, y], own_sem)
    own.start()
    pl.semaphore_wait(pltpu.get_barrier_semaphore(), 2 + (z < planes - 1).astype(jnp.int32))

    def up(s):
        src = kv_ref if s == 0 else all_ref.at[z - s, c, y]
        return remote(src, all_ref.at[z - s, c, y], z_send.at[s], z_recv.at[s + 1], me + 4)

    def from_below(s):
        slot = all_ref.at[z - s, c, y]
        return remote(slot, slot, z_send.at[s], z_recv.at[s], me)

    def across(s):
        src = kv_ref if s == 0 else all_ref.at[z - s, c, y]
        return remote(src, all_ref.at[z - s, c, y], y_send.at[s], y_recv.at[s], side)

    def between(s):
        pair = all_ref.at[z - s, c]
        return remote(pair, pair, c_send.at[s], c_recv.at[s], sibling)

    for s in range(planes + 1):
        if s < planes:

            @pl.when(z >= s)
            def _(s=s):
                if s > 0:
                    from_below(s).wait_recv()
                if s < planes - 1:

                    @pl.when(z < planes - 1)
                    def _():
                        up(s).start()

                across(s).start()

        if s == 0:
            own.wait()
        else:

            @pl.when(z >= s - 1)
            def _(s=s):
                across(s - 1).wait_recv()
                between(s - 1).start()

    for s in range(planes):

        @pl.when(z >= s)
        def _(s=s):
            if s < planes - 1:

                @pl.when(z < planes - 1)
                def _():
                    up(s).wait_send()

            across(s).wait_send()
            between(s).wait()


def gather_blocks(kv, planes):
    shape = (planes, 2, 2) + kv.shape
    dma = pltpu.SemaphoreType.DMA
    return pl.pallas_call(
        functools.partial(gather_kernel, planes),
        out_shape=jax.ShapeDtypeStruct(shape, kv.dtype),
        in_specs=[pl.BlockSpec(memory_space=pl.ANY)],
        out_specs=pl.BlockSpec(memory_space=pl.ANY),
        scratch_shapes=[dma(())] + [dma((planes,))] * 6,
        compiler_params=pltpu.CompilerParams(collective_id=0, has_side_effects=True),
        name="gather_blocks",
    )(kv)


def attend_kernel(
    chosen_ref, usable_ref, q_ref, do_ref, o_ref, lse_ref, kv_ref,
    dq_ref, part_ref, delta, dq_sum,
):
    slot = pl.program_id(0)
    heads = q_ref.shape[1] // HD

    def columns(h):
        return slice(h * HD, (h + 1) * HD)

    @pl.when(slot == 0)
    def _():
        part_ref[...] = jnp.zeros_like(part_ref)
        dq_sum[...] = jnp.zeros_like(dq_sum)
        for h in range(heads):
            product = do_ref[:, columns(h)].astype(jnp.float32) * o_ref[:, columns(h)].astype(jnp.float32)
            delta[h : h + 1, :] = jnp.sum(product.T, axis=0, keepdims=True)

    def pair(diagonal):
        key = kv_ref[0, 0, 0, :, :HD]
        value = kv_ref[0, 0, 0, :, HD:]
        key_t = key.astype(jnp.float32).T.astype(jnp.bfloat16)
        if diagonal:
            key_pos = lax.broadcasted_iota(jnp.int32, (BLOCK, BLOCK), 0)
            query_pos = lax.broadcasted_iota(jnp.int32, (BLOCK, BLOCK), 1)
            seen = key_pos <= query_pos
        dk = jnp.zeros((BLOCK, HD), jnp.float32)
        dv = jnp.zeros((BLOCK, HD), jnp.float32)
        for h in range(heads):
            query, cotangent = q_ref[:, columns(h)], do_ref[:, columns(h)]
            scores = lax.dot_general(key, query, NT, preferred_element_type=jnp.float32)
            probs = jnp.exp2(scores * (SCALE * LOG2E) - lse_ref[h : h + 1, :] * LOG2E)
            if diagonal:
                probs = jnp.where(seen, probs, 0.0)
            prob_grad = lax.dot_general(value, cotangent, NT, preferred_element_type=jnp.float32)
            score_half = (probs * (prob_grad - delta[h : h + 1, :])).astype(jnp.bfloat16)
            probs_half = probs.astype(jnp.bfloat16)
            dv = dv + lax.dot_general(probs_half, cotangent, NN, preferred_element_type=jnp.float32)
            dk = dk + lax.dot_general(score_half, query, NN, preferred_element_type=jnp.float32)
            dq_sum[h] += lax.dot_general(key_t, score_half, NN, preferred_element_type=jnp.float32)
        block = chosen_ref[slot]
        at = (block // 4, block % 2, (block // 2) % 2)
        part_ref[at + (slice(None), slice(0, HD))] = (dk * SCALE).astype(jnp.bfloat16)
        part_ref[at + (slice(None), slice(HD, 2 * HD))] = dv.astype(jnp.bfloat16)

    @pl.when(slot == 0)
    def _():
        pair(True)

    @pl.when((slot > 0) & (usable_ref[slot] > 0))
    def _():
        pair(False)

    @pl.when(slot == TOPK)
    def _():
        for h in range(heads):
            dq_ref[:, columns(h)] = (dq_sum[h] * SCALE).T.astype(jnp.bfloat16)


def attend(chosen, usable, queries, output_grad, output_rows, lse, blocks):
    rows, width = queries.shape
    heads = width // HD
    whole = lambda s, chosen, usable: (0, 0)
    wide = pl.BlockSpec((rows, width), whole)
    return pl.pallas_call(
        attend_kernel,
        out_shape=(
            jax.ShapeDtypeStruct((rows, width), jnp.bfloat16),
            jax.ShapeDtypeStruct(blocks.shape, jnp.bfloat16),
        ),
        grid_spec=pltpu.PrefetchScalarGridSpec(
            num_scalar_prefetch=2,
            grid=(TOPK + 1,),
            in_specs=[
                wide, wide, wide,
                pl.BlockSpec((heads, rows), whole),
                pl.BlockSpec(
                    (1, 1, 1) + blocks.shape[3:],
                    lambda s, chosen, usable: (
                        chosen[s] // 4, chosen[s] % 2, (chosen[s] // 2) % 2, 0, 0,
                    ),
                ),
            ],
            out_specs=[wide, pl.BlockSpec(blocks.shape, lambda s, chosen, usable: (0,) * 5)],
            scratch_shapes=[
                pltpu.VMEM((heads, rows), jnp.float32),
                pltpu.VMEM((heads, HD, rows), jnp.float32),
            ],
        ),
        compiler_params=pltpu.CompilerParams(vmem_limit_bytes=VMEM_LIMIT),
        cost_estimate=pl.CostEstimate(flops=6 * 10**9, bytes_accessed=10 * 2**20, transcendentals=4 * 2**20),
        name="attend",
    )(chosen, usable, queries, output_grad, output_rows, lse, blocks)


def scatter_kernel(
    planes, part_ref, out_ref, c_in, y_in, z_in, y_out, z_out, held,
    z_send, z_recv, y_send, y_recv, c_send, c_recv,
):
    me, z, y, c = place()
    sibling, side = sibling_of(me, c), beside(me, y)
    greet(sibling)
    greet(side)

    @pl.when(z < planes - 1)
    def _():
        greet(me + 4)

    pl.semaphore_wait(pltpu.get_barrier_semaphore(), 2 + (z > 0).astype(jnp.int32))

    def between(t):
        return remote(part_ref.at[t, 1 - c], c_in.at[t], c_send.at[t], c_recv.at[t], sibling)

    def across(t):
        return remote(y_out.at[t], y_in.at[t], y_send.at[t], y_recv.at[t], side)

    def down(t):
        return remote(z_out.at[t], z_in.at[t], z_send.at[t], z_recv.at[t], me - 4)

    for t in range(planes):

        @pl.when(t <= z)
        def _(t=t):
            between(t).start()

    for t in range(planes):

        @pl.when(t <= z)
        def _(t=t):
            between(t).wait_recv()
            y_out[t] = (
                part_ref[t, c, 1 - y].astype(jnp.float32) + c_in[t, 1 - y].astype(jnp.float32)
            ).astype(jnp.bfloat16)
            across(t).start()
            held[t] = part_ref[t, c, y].astype(jnp.float32) + c_in[t, y].astype(jnp.float32)

    for t in range(planes):

        @pl.when(t <= z)
        def _(t=t):
            across(t).wait_recv()
            held[t] += y_in[t].astype(jnp.float32)

            @pl.when(z < planes - 1)
            def _():
                down(t).wait_recv()
                held[t] += z_in[t].astype(jnp.float32)

            @pl.when(t < z)
            def _():
                z_out[t] = held[t].astype(jnp.bfloat16)
                down(t).start()

            @pl.when(t == z)
            def _():
                out_ref[...] = held[t].astype(jnp.bfloat16)

    for t in range(planes):

        @pl.when(t <= z)
        def _(t=t):
            between(t).wait_send()
            across(t).wait_send()

            @pl.when(t < z)
            def _():
                down(t).wait_send()


def scatter_blocks(part, planes):
    block = part.shape[3:]
    dma = pltpu.SemaphoreType.DMA
    slots = pltpu.VMEM((planes,) + block, jnp.bfloat16)
    return pl.pallas_call(
        functools.partial(scatter_kernel, planes),
        out_shape=jax.ShapeDtypeStruct(block, jnp.bfloat16),
        in_specs=[pl.BlockSpec(memory_space=pltpu.VMEM)],
        out_specs=pl.BlockSpec(memory_space=pltpu.VMEM),
        scratch_shapes=[
            pltpu.VMEM((planes, 2) + block, jnp.bfloat16),
            slots, slots, slots, slots,
            pltpu.VMEM((planes,) + block, jnp.float32),
        ] + [dma((planes,))] * 6,
        compiler_params=pltpu.CompilerParams(
            collective_id=1, has_side_effects=True, vmem_limit_bytes=VMEM_LIMIT
        ),
        cost_estimate=pl.CostEstimate(flops=10**9, bytes_accessed=100 * 2**20, transcendentals=0),
        name="scatter_blocks",
    )(part)


TILE = 256


def project_kernel(
    where_ref, dq_ref, dkv_ref, dq_far_ref, dkv_far_ref, wq_ref, wk_ref, wv_ref, near_ref, far_ref, out_ref
):
    step, half = pl.program_id(0), pl.num_programs(0) // 2
    feature = dq_ref.shape[1]

    def dot(lhs, rhs):
        return lax.dot_general(lhs, rhs, NT, preferred_element_type=jnp.float32)

    total = dot(dq_ref[...], wq_ref[...])
    total += dot(dkv_ref[:, :HD], wk_ref[...])
    total += dot(dkv_ref[:, HD:], wv_ref[...])
    weights = jnp.where(step < half, near_ref[...], far_ref[...])
    total += dot(dq_far_ref[...], weights[:, :feature])
    total += dot(dkv_far_ref[...], weights[:, feature:])
    out_ref[...] = total.astype(jnp.bfloat16)


def project(dq, dkv, dq_far, dkv_far, wq, wk, wv, near, far):
    rows = dq.shape[0]
    half = near.shape[0] // TILE
    where = jnp.stack([lax.axis_index("grp"), lax.axis_index("ctx") % 2]).astype(jnp.int32)

    def column(i, where):
        core = jnp.where(i < half, where[1], 1 - where[1])
        return core * half + i % half

    def whole(array):
        return pl.BlockSpec(array.shape, lambda i, where: (0, 0))

    def mine(array):
        return pl.BlockSpec(
            (TILE, array.shape[1]), lambda i, where: (where[0] * 2 * half + column(i, where), 0)
        )

    return pl.pallas_call(
        project_kernel,
        out_shape=jax.ShapeDtypeStruct((rows, 2 * half * TILE), jnp.bfloat16),
        grid_spec=pltpu.PrefetchScalarGridSpec(
            num_scalar_prefetch=1,
            grid=(2 * half,),
            in_specs=[
                whole(dq), whole(dkv), whole(dq_far), whole(dkv_far), mine(wq), mine(wk), mine(wv),
                pl.BlockSpec((TILE, near.shape[1]), lambda i, where: (jnp.minimum(i, half - 1), 0)),
                pl.BlockSpec((TILE, near.shape[1]), lambda i, where: (jnp.maximum(i - half, 0), 0)),
            ],
            out_specs=pl.BlockSpec((rows, TILE), lambda i, where: (0, column(i, where))),
        ),
        compiler_params=pltpu.CompilerParams(vmem_limit_bytes=VMEM_LIMIT),
        name="project",
    )(where, dq, dkv, dq_far, dkv_far, wq, wk, wv, near, far)


def on_device(
    queries, key_rows, value_rows, output_rows, output_grad, log_normalizer,
    selection, query_weight, key_weight, value_weight,
):
    position = lax.axis_index("ctx")
    contexts = lax.axis_size("ctx")
    groups = lax.axis_size("grp")
    planes = contexts // 4
    paired = groups == 2

    if paired:
        group, core = lax.axis_index("grp"), position % 2
        share = query_weight.shape[0] // 4
        start = (1 - group) * 2 * share + core * share
        swap = [(0, 1), (1, 0)]
        siblings = [(i, i ^ 1) for i in range(contexts)]
        outgoing = jnp.concatenate(
            [
                lax.dynamic_slice_in_dim(weight, start, share, 0)
                for weight in (query_weight, key_weight, value_weight)
            ],
            axis=1,
        )
        near = lax.ppermute(outgoing, "grp", swap)
        far = lax.ppermute(near, "ctx", siblings)

    blocks = gather_blocks(jnp.concatenate([key_rows, value_rows], axis=1), planes)
    row = lax.dynamic_index_in_dim(selection, position, 0, keepdims=False).astype(jnp.int32)
    chosen = jnp.concatenate([position[None].astype(jnp.int32), row])
    usable = jnp.concatenate([jnp.ones((1,), jnp.int32), (row < position).astype(jnp.int32)])
    grad_query, part = attend(
        chosen, usable, queries, output_grad, output_rows, log_normalizer.T, blocks
    )
    if paired:
        query_far = lax.ppermute(grad_query, "grp", swap)
    grad_keyval = scatter_blocks(part, planes)
    if paired:
        keyval_far = lax.ppermute(grad_keyval, "grp", swap)
        return project(
            grad_query, grad_keyval, query_far, keyval_far,
            query_weight, key_weight, value_weight, near, far,
        )
    dot = functools.partial(lax.dot_general, dimension_numbers=NT, preferred_element_type=jnp.float32)
    combined = dot(grad_query, query_weight)
    combined = combined + dot(grad_keyval[:, :HD], key_weight)
    combined = combined + dot(grad_keyval[:, HD:], value_weight)
    return lax.psum_scatter(combined.astype(jnp.bfloat16), "grp", scatter_dimension=1, tiled=True)


def solution(mesh):
    return jax.shard_map(
        on_device,
        mesh=mesh,
        in_specs=(
            P("ctx", "grp"),
            P("ctx", "grp"),
            P("ctx", "grp"),
            P("ctx", "grp"),
            P("ctx", "grp"),
            P("ctx", "grp"),
            P(),
            P(None, "grp"),
            P(None, "grp"),
            P(None, "grp"),
        ),
        out_specs=P("ctx", "grp"),
        check_vma=False,
    )
```

```python
import functools
import math

import jax
import jax.numpy as jnp
from jax import lax
from jax.experimental import pallas as pl
from jax.experimental.pallas import tpu as pltpu
from jax.sharding import PartitionSpec as P

HD = 128
BLOCK = 512
TOPK = 3
MESH = pl.DeviceIdType.MESH
SCALE = float(HD) ** (-0.5)
LOG2E = math.log2(math.e)
VMEM_LIMIT = 56 * 1024 * 1024
NT = (((1,), (1,)), ((), ()))
NN = (((1,), (0,)), ((), ()))


def place():
    me = lax.axis_index("ctx")
    return me, me // 4, (me // 2) % 2, me % 2


def sibling_of(me, core):
    return me + 1 - 2 * core


def beside(me, column):
    return me + 2 - 4 * column


def remote(src, dst, send, recv, target):
    return pltpu.make_async_remote_copy(
        src_ref=src, dst_ref=dst, send_sem=send, recv_sem=recv,
        device_id={"ctx": target}, device_id_type=MESH,
    )


def greet(target):
    pl.semaphore_signal(
        pltpu.get_barrier_semaphore(), inc=1, device_id={"ctx": target}, device_id_type=MESH
    )


def gather_kernel(planes, kv_ref, all_ref, own_sem, z_send, z_recv, y_send, y_recv, c_send, c_recv):
    me, z, y, c = place()
    sibling, side = sibling_of(me, c), beside(me, y)
    greet(sibling)
    greet(side)

    @pl.when(z > 0)
    def _():
        greet(me - 4)

    own = pltpu.make_async_copy(kv_ref, all_ref.at[z, c, y], own_sem)
    own.start()
    pl.semaphore_wait(pltpu.get_barrier_semaphore(), 2 + (z < planes - 1).astype(jnp.int32))

    def up(s):
        src = kv_ref if s == 0 else all_ref.at[z - s, c, y]
        return remote(src, all_ref.at[z - s, c, y], z_send.at[s], z_recv.at[s + 1], me + 4)

    def from_below(s):
        slot = all_ref.at[z - s, c, y]
        return remote(slot, slot, z_send.at[s], z_recv.at[s], me)

    def across(s):
        src = kv_ref if s == 0 else all_ref.at[z - s, c, y]
        return remote(src, all_ref.at[z - s, c, y], y_send.at[s], y_recv.at[s], side)

    def between(s):
        pair = all_ref.at[z - s, c]
        return remote(pair, pair, c_send.at[s], c_recv.at[s], sibling)

    for s in range(planes + 1):
        if s < planes:

            @pl.when(z >= s)
            def _(s=s):
                if s > 0:
                    from_below(s).wait_recv()
                if s < planes - 1:

                    @pl.when(z < planes - 1)
                    def _():
                        up(s).start()

                across(s).start()

        if s == 0:
            own.wait()
        else:

            @pl.when(z >= s - 1)
            def _(s=s):
                across(s - 1).wait_recv()
                between(s - 1).start()

    for s in range(planes):

        @pl.when(z >= s)
        def _(s=s):
            if s < planes - 1:

                @pl.when(z < planes - 1)
                def _():
                    up(s).wait_send()

            across(s).wait_send()
            between(s).wait()


def gather_blocks(kv, planes):
    shape = (planes, 2, 2) + kv.shape
    dma = pltpu.SemaphoreType.DMA
    return pl.pallas_call(
        functools.partial(gather_kernel, planes),
        out_shape=jax.ShapeDtypeStruct(shape, kv.dtype),
        in_specs=[pl.BlockSpec(memory_space=pl.ANY)],
        out_specs=pl.BlockSpec(memory_space=pl.ANY),
        scratch_shapes=[dma(())] + [dma((planes,))] * 6,
        compiler_params=pltpu.CompilerParams(collective_id=0, has_side_effects=True),
        name="gather_blocks",
    )(kv)


def attend_kernel(
    chosen_ref, usable_ref, q_ref, do_ref, o_ref, lse_ref, kv_ref,
    dq_ref, part_ref, delta, dq_sum,
):
    slot = pl.program_id(0)
    heads = q_ref.shape[1] // HD

    def columns(h):
        return slice(h * HD, (h + 1) * HD)

    @pl.when(slot == 0)
    def _():
        part_ref[...] = jnp.zeros_like(part_ref)
        dq_sum[...] = jnp.zeros_like(dq_sum)
        for h in range(heads):
            product = do_ref[:, columns(h)].astype(jnp.float32) * o_ref[:, columns(h)].astype(jnp.float32)
            delta[h : h + 1, :] = jnp.sum(product.T, axis=0, keepdims=True)

    def pair(diagonal):
        key = kv_ref[0, 0, 0, :, :HD]
        value = kv_ref[0, 0, 0, :, HD:]
        key_t = key.astype(jnp.float32).T.astype(jnp.bfloat16)
        if diagonal:
            key_pos = lax.broadcasted_iota(jnp.int32, (BLOCK, BLOCK), 0)
            query_pos = lax.broadcasted_iota(jnp.int32, (BLOCK, BLOCK), 1)
            seen = key_pos <= query_pos
        dk = jnp.zeros((BLOCK, HD), jnp.float32)
        dv = jnp.zeros((BLOCK, HD), jnp.float32)
        for h in range(heads):
            query, cotangent = q_ref[:, columns(h)], do_ref[:, columns(h)]
            scores = lax.dot_general(key, query, NT, preferred_element_type=jnp.float32)
            probs = jnp.exp2(scores * (SCALE * LOG2E) - lse_ref[h : h + 1, :] * LOG2E)
            if diagonal:
                probs = jnp.where(seen, probs, 0.0)
            prob_grad = lax.dot_general(value, cotangent, NT, preferred_element_type=jnp.float32)
            score_half = (probs * (prob_grad - delta[h : h + 1, :])).astype(jnp.bfloat16)
            probs_half = probs.astype(jnp.bfloat16)
            dv = dv + lax.dot_general(probs_half, cotangent, NN, preferred_element_type=jnp.float32)
            dk = dk + lax.dot_general(score_half, query, NN, preferred_element_type=jnp.float32)
            dq_sum[h] += lax.dot_general(key_t, score_half, NN, preferred_element_type=jnp.float32)
        block = chosen_ref[slot]
        at = (block // 4, block % 2, (block // 2) % 2)
        part_ref[at + (slice(None), slice(0, HD))] = (dk * SCALE).astype(jnp.bfloat16)
        part_ref[at + (slice(None), slice(HD, 2 * HD))] = dv.astype(jnp.bfloat16)

    @pl.when(slot == 0)
    def _():
        pair(True)

    @pl.when((slot > 0) & (usable_ref[slot] > 0))
    def _():
        pair(False)

    @pl.when(slot == TOPK)
    def _():
        for h in range(heads):
            dq_ref[:, columns(h)] = (dq_sum[h] * SCALE).T.astype(jnp.bfloat16)


def attend(chosen, usable, queries, output_grad, output_rows, lse, blocks):
    rows, width = queries.shape
    heads = width // HD
    whole = lambda s, chosen, usable: (0, 0)
    wide = pl.BlockSpec((rows, width), whole)
    return pl.pallas_call(
        attend_kernel,
        out_shape=(
            jax.ShapeDtypeStruct((rows, width), jnp.bfloat16),
            jax.ShapeDtypeStruct(blocks.shape, jnp.bfloat16),
        ),
        grid_spec=pltpu.PrefetchScalarGridSpec(
            num_scalar_prefetch=2,
            grid=(TOPK + 1,),
            in_specs=[
                wide, wide, wide,
                pl.BlockSpec((heads, rows), whole),
                pl.BlockSpec(
                    (1, 1, 1) + blocks.shape[3:],
                    lambda s, chosen, usable: (
                        chosen[s] // 4, chosen[s] % 2, (chosen[s] // 2) % 2, 0, 0,
                    ),
                ),
            ],
            out_specs=[wide, pl.BlockSpec(blocks.shape, lambda s, chosen, usable: (0,) * 5)],
            scratch_shapes=[
                pltpu.VMEM((heads, rows), jnp.float32),
                pltpu.VMEM((heads, HD, rows), jnp.float32),
            ],
        ),
        compiler_params=pltpu.CompilerParams(vmem_limit_bytes=VMEM_LIMIT),
        cost_estimate=pl.CostEstimate(flops=6 * 10**9, bytes_accessed=10 * 2**20, transcendentals=4 * 2**20),
        name="attend",
    )(chosen, usable, queries, output_grad, output_rows, lse, blocks)


def scatter_kernel(
    planes, part_ref, out_ref, c_in, y_in, z_in, y_out, z_out, held,
    z_send, z_recv, y_send, y_recv, c_send, c_recv,
):
    me, z, y, c = place()
    sibling, side = sibling_of(me, c), beside(me, y)
    greet(sibling)
    greet(side)

    @pl.when(z < planes - 1)
    def _():
        greet(me + 4)

    pl.semaphore_wait(pltpu.get_barrier_semaphore(), 2 + (z > 0).astype(jnp.int32))

    def between(t):
        return remote(part_ref.at[t, 1 - c], c_in.at[t], c_send.at[t], c_recv.at[t], sibling)

    def across(t):
        return remote(y_out.at[t], y_in.at[t], y_send.at[t], y_recv.at[t], side)

    def down(t):
        return remote(z_out.at[t], z_in.at[t], z_send.at[t], z_recv.at[t], me - 4)

    for t in range(planes):

        @pl.when(t <= z)
        def _(t=t):
            between(t).start()

    for t in range(planes):

        @pl.when(t <= z)
        def _(t=t):
            between(t).wait_recv()
            y_out[t] = (
                part_ref[t, c, 1 - y].astype(jnp.float32) + c_in[t, 1 - y].astype(jnp.float32)
            ).astype(jnp.bfloat16)
            across(t).start()
            held[t] = part_ref[t, c, y].astype(jnp.float32) + c_in[t, y].astype(jnp.float32)

    for t in range(planes):

        @pl.when(t <= z)
        def _(t=t):
            across(t).wait_recv()
            held[t] += y_in[t].astype(jnp.float32)

            @pl.when(z < planes - 1)
            def _():
                down(t).wait_recv()
                held[t] += z_in[t].astype(jnp.float32)

            @pl.when(t < z)
            def _():
                z_out[t] = held[t].astype(jnp.bfloat16)
                down(t).start()

            @pl.when(t == z)
            def _():
                out_ref[...] = held[t].astype(jnp.bfloat16)

    for t in range(planes):

        @pl.when(t <= z)
        def _(t=t):
            between(t).wait_send()
            across(t).wait_send()

            @pl.when(t < z)
            def _():
                down(t).wait_send()


def scatter_blocks(part, planes):
    block = part.shape[3:]
    dma = pltpu.SemaphoreType.DMA
    slots = pltpu.VMEM((planes,) + block, jnp.bfloat16)
    return pl.pallas_call(
        functools.partial(scatter_kernel, planes),
        out_shape=jax.ShapeDtypeStruct(block, jnp.bfloat16),
        in_specs=[pl.BlockSpec(memory_space=pltpu.VMEM)],
        out_specs=pl.BlockSpec(memory_space=pltpu.VMEM),
        scratch_shapes=[
            pltpu.VMEM((planes, 2) + block, jnp.bfloat16),
            slots, slots, slots, slots,
            pltpu.VMEM((planes,) + block, jnp.float32),
        ] + [dma((planes,))] * 6,
        compiler_params=pltpu.CompilerParams(
            collective_id=1, has_side_effects=True, vmem_limit_bytes=VMEM_LIMIT
        ),
        cost_estimate=pl.CostEstimate(flops=10**9, bytes_accessed=100 * 2**20, transcendentals=0),
        name="scatter_blocks",
    )(part)


def toward(src, dst, send, recv):
    return pltpu.make_async_remote_copy(
        src_ref=src, dst_ref=dst, send_sem=send, recv_sem=recv,
        device_id={"grp": 1 - lax.axis_index("grp")}, device_id_type=MESH,
    )


def greet_group():
    pl.semaphore_signal(
        pltpu.get_barrier_semaphore(), inc=1,
        device_id={"grp": 1 - lax.axis_index("grp")}, device_id_type=MESH,
    )


def columns(h):
    return slice(h * HD, (h + 1) * HD)


def block_gradients(key, value, q_ref, do_ref, lse_ref, delta_ref, dq_sum, diagonal):
    heads = q_ref.shape[1] // HD
    key_t = key.astype(jnp.float32).T.astype(jnp.bfloat16)
    if diagonal:
        key_pos = lax.broadcasted_iota(jnp.int32, (BLOCK, BLOCK), 0)
        query_pos = lax.broadcasted_iota(jnp.int32, (BLOCK, BLOCK), 1)
        seen = key_pos <= query_pos
    dk = jnp.zeros((BLOCK, HD), jnp.float32)
    dv = jnp.zeros((BLOCK, HD), jnp.float32)
    for h in range(heads):
        query, cotangent = q_ref[:, columns(h)], do_ref[:, columns(h)]
        scores = lax.dot_general(key, query, NT, preferred_element_type=jnp.float32)
        probs = jnp.exp2(scores * (SCALE * LOG2E) - lse_ref[h : h + 1, :] * LOG2E)
        if diagonal:
            probs = jnp.where(seen, probs, 0.0)
        prob_grad = lax.dot_general(value, cotangent, NT, preferred_element_type=jnp.float32)
        score_half = (probs * (prob_grad - delta_ref[h : h + 1, :])).astype(jnp.bfloat16)
        probs_half = probs.astype(jnp.bfloat16)
        dv = dv + lax.dot_general(probs_half, cotangent, NN, preferred_element_type=jnp.float32)
        dk = dk + lax.dot_general(score_half, query, NN, preferred_element_type=jnp.float32)
        dq = lax.dot_general(key_t, score_half, NN, preferred_element_type=jnp.float32)
        dq_sum[h] = dq if diagonal else dq_sum[h] + dq
    return (dk * SCALE).astype(jnp.bfloat16), dv.astype(jnp.bfloat16)


def open_kernel(
    planes, key_ref, value_ref, q_ref, do_ref, o_ref, lse_ref, wq_ref, wk_ref, wv_ref,
    all_ref, near_ref, dq_ref, delta_ref, known_ref,
    kv, prev, own_sem, prev_sem, w_send, w_recv, z_send, z_recv, y_send, y_recv, c_send, c_recv,
):
    me, z, y, c = place()
    group = lax.axis_index("grp")
    sibling, side = sibling_of(me, c), beside(me, y)
    greet(sibling)
    greet(side)
    greet_group()

    @pl.when(z > 0)
    def _():
        greet(me - 4)

    kv[0] = key_ref[...]
    kv[1] = value_ref[...]
    own = pltpu.make_async_copy(kv, all_ref.at[z, c, y], own_sem)
    own.start()
    pl.semaphore_wait(pltpu.get_barrier_semaphore(), 3 + (z < planes - 1).astype(jnp.int32))

    share = near_ref.shape[0]
    rows = pl.ds(pl.multiple_of((1 - group) * 2 * share + c * share, share), share)
    weights = []
    first = 0
    for i, weight in enumerate((wq_ref, wk_ref, wv_ref)):
        width = weight.shape[1]
        weights.append(
            toward(weight.at[rows], near_ref.at[:, first : first + width], w_send.at[i], w_recv.at[i])
        )
        first += width

    def up(s):
        src = kv if s == 0 else all_ref.at[z - s, c, y]
        return remote(src, all_ref.at[z - s, c, y], z_send.at[s], z_recv.at[s + 1], me + 4)

    def from_below(s):
        slot = all_ref.at[z - s, c, y]
        return remote(slot, slot, z_send.at[s], z_recv.at[s], me)

    def across(s):
        src = kv if s == 0 else all_ref.at[z - s, c, y]
        return remote(src, all_ref.at[z - s, c, y], y_send.at[s], y_recv.at[s], side)

    def between(s):
        pair = all_ref.at[z - s, c]
        return remote(pair, pair, c_send.at[s], c_recv.at[s], sibling)

    for s in range(planes + 1):
        if s < planes:

            @pl.when(z >= s)
            def _(s=s):
                if s > 0:
                    from_below(s).wait_recv()
                if s < planes - 1:

                    @pl.when(z < planes - 1)
                    def _():
                        up(s).start()

                across(s).start()

        if s == 0:
            for copy in weights:
                copy.start()
            for h in range(q_ref.shape[1] // HD):
                product = do_ref[:, columns(h)].astype(jnp.float32) * o_ref[:, columns(h)].astype(jnp.float32)
                delta_ref[h : h + 1, :] = jnp.sum(product.T, axis=0, keepdims=True)
            dk, dv = block_gradients(kv[0], kv[1], q_ref, do_ref, lse_ref, delta_ref, dq_ref, True)
            known_ref[0, 0] = dk
            known_ref[0, 1] = dv
            own.wait()
        else:

            @pl.when(z >= s - 1)
            def _(s=s):
                across(s - 1).wait_recv()
                between(s - 1).start()

        if s == 2:
            between(0).wait_recv()

            @pl.when(z >= 1)
            def _():
                between(1).wait_recv()

            @pl.when(me > 0)
            def _():
                last = me - 1
                fetch = pltpu.make_async_copy(
                    all_ref.at[last // 4, last % 2, (last // 2) % 2], prev, prev_sem
                )
                fetch.start()
                fetch.wait()
                dk, dv = block_gradients(prev[0], prev[1], q_ref, do_ref, lse_ref, delta_ref, dq_ref, False)
                known_ref[1, 0] = dk
                known_ref[1, 1] = dv

    for s in range(planes):

        @pl.when(z >= s)
        def _(s=s):
            if s < planes - 1:

                @pl.when(z < planes - 1)
                def _():
                    up(s).wait_send()

            across(s).wait_send()
            between(s).wait_send()
            if s > 1:
                between(s).wait_recv()

    for copy in weights:
        copy.wait()


def open_blocks(key, value, queries, output_grad, output_rows, lse, weights, planes):
    rows, width = queries.shape
    heads = width // HD
    block = (2,) + key.shape
    share = (weights[0].shape[0] // 4, sum(weight.shape[1] for weight in weights))
    dma = pltpu.SemaphoreType.DMA
    vmem = pl.BlockSpec(memory_space=pltpu.VMEM)
    anywhere = pl.BlockSpec(memory_space=pl.ANY)
    return pl.pallas_call(
        functools.partial(open_kernel, planes),
        out_shape=(
            jax.ShapeDtypeStruct((planes, 2, 2) + block, jnp.bfloat16),
            jax.ShapeDtypeStruct(share, jnp.bfloat16),
            jax.ShapeDtypeStruct((heads, HD, rows), jnp.float32),
            jax.ShapeDtypeStruct((heads, rows), jnp.float32),
            jax.ShapeDtypeStruct((2,) + block, jnp.bfloat16),
        ),
        in_specs=[vmem] * 6 + [anywhere] * 3,
        out_specs=(anywhere, anywhere, vmem, vmem, vmem),
        scratch_shapes=[
            pltpu.VMEM(block, jnp.bfloat16), pltpu.VMEM(block, jnp.bfloat16),
            dma(()), dma(()), dma((3,)), dma((3,)),
        ] + [dma((planes,))] * 6,
        compiler_params=pltpu.CompilerParams(
            collective_id=2, has_side_effects=True, vmem_limit_bytes=VMEM_LIMIT
        ),
        name="open_blocks",
    )(key, value, queries, output_grad, output_rows, lse, *weights)


def chosen_kernel(
    selection_ref, q_ref, do_ref, lse_ref, delta_ref, dq_in_ref, known_ref, all_ref,
    dq_ref, part_ref, fetched, dq_sum, sems,
):
    me = lax.axis_index("ctx")
    picks = [selection_ref[me, column] for column in range(TOPK)]
    others = [
        jnp.where(picks[0] == me - 1, picks[1], picks[0]),
        jnp.where(picks[2] == me - 1, picks[1], picks[2]),
    ]

    def at(block):
        return (block // 4, block % 2, (block // 2) % 2)

    copies = [
        pltpu.make_async_copy(all_ref.at[at(block)], fetched.at[i], sems.at[i])
        for i, block in enumerate(others)
    ]
    for copy in copies:
        copy.start()
    part_ref[...] = jnp.zeros_like(part_ref)
    dq_sum[...] = dq_in_ref[...]
    part_ref[at(me)] = known_ref[0]

    @pl.when(me > 0)
    def _():
        part_ref[at(me - 1)] = known_ref[1]

    for i, block in enumerate(others):
        copies[i].wait()

        @pl.when(block < me)
        def _(i=i, block=block):
            dk, dv = block_gradients(
                fetched[i, 0], fetched[i, 1], q_ref, do_ref, lse_ref, delta_ref, dq_sum, False
            )
            part_ref[at(block) + (0,)] = dk
            part_ref[at(block) + (1,)] = dv

    for h in range(q_ref.shape[1] // HD):
        dq_ref[:, columns(h)] = (dq_sum[h] * SCALE).T.astype(jnp.bfloat16)


def chosen_blocks(selection, queries, output_grad, lse, delta, dq, known, blocks):
    vmem = pl.BlockSpec(memory_space=pltpu.VMEM)
    return pl.pallas_call(
        chosen_kernel,
        out_shape=(
            jax.ShapeDtypeStruct(queries.shape, jnp.bfloat16),
            jax.ShapeDtypeStruct(blocks.shape, jnp.bfloat16),
        ),
        in_specs=[pl.BlockSpec(memory_space=pltpu.SMEM)] + [vmem] * 6 + [pl.BlockSpec(memory_space=pl.ANY)],
        out_specs=(vmem, vmem),
        scratch_shapes=[
            pltpu.VMEM((2,) + blocks.shape[3:], jnp.bfloat16),
            pltpu.VMEM(dq.shape, jnp.float32),
            pltpu.SemaphoreType.DMA((2,)),
        ],
        compiler_params=pltpu.CompilerParams(vmem_limit_bytes=VMEM_LIMIT),
        name="chosen_blocks",
    )(selection, queries, output_grad, lse, delta, dq, known, blocks)


TILE = 256


def close_kernel(
    planes, part_ref, dq_ref, near_ref, wq_ref, wk_ref, wv_ref, out_ref,
    c_in, y_in, z_in, y_out, z_out, held, mine, theirs, dq_far, dkv, dkv_far, total,
    z_send, z_recv, y_send, y_recv, c_send, c_recv, local_sem, w_send, w_recv, x_send, x_recv,
):
    me, z, y, c = place()
    group = lax.axis_index("grp")
    sibling, side = sibling_of(me, c), beside(me, y)
    greet(sibling)
    greet(side)
    greet_group()

    @pl.when(z < planes - 1)
    def _():
        greet(me + 4)

    half = out_ref.shape[1]
    share = half // 2
    feature = dq_ref.shape[1]
    rows = pl.ds(pl.multiple_of(group * half, half), half)
    locals_ = [pltpu.make_async_copy(near_ref, theirs.at[c], local_sem.at[0])]
    first = 0
    for i, weight in enumerate((wq_ref, wk_ref, wv_ref)):
        width = weight.shape[1]
        locals_.append(
            pltpu.make_async_copy(weight.at[rows], mine.at[:, first : first + width], local_sem.at[i + 1])
        )
        first += width
    for copy in locals_:
        copy.start()

    pl.semaphore_wait(pltpu.get_barrier_semaphore(), 3 + (z > 0).astype(jnp.int32))

    def between(t):
        return remote(part_ref.at[t, 1 - c], c_in.at[t], c_send.at[t], c_recv.at[t], sibling)

    def across(t):
        return remote(y_out.at[t], y_in.at[t], y_send.at[t], y_recv.at[t], side)

    def down(t):
        return remote(z_out.at[t], z_in.at[t], z_send.at[t], z_recv.at[t], me - 4)

    query_swap = toward(dq_ref, dq_far, x_send.at[0], x_recv.at[0])
    keyval_swap = toward(dkv, dkv_far, x_send.at[1], x_recv.at[1])
    weight_swap = remote(near_ref, theirs.at[c], w_send, w_recv, sibling)

    for t in range(planes):

        @pl.when(t <= z)
        def _(t=t):
            between(t).start()

    query_swap.start()
    weight_swap.start()

    for t in range(planes):

        @pl.when(t <= z)
        def _(t=t):
            between(t).wait_recv()
            y_out[t] = (
                part_ref[t, c, 1 - y].astype(jnp.float32) + c_in[t, 1 - y].astype(jnp.float32)
            ).astype(jnp.bfloat16)
            across(t).start()
            held[t] = part_ref[t, c, y].astype(jnp.float32) + c_in[t, y].astype(jnp.float32)

    def dot(lhs, rhs):
        return lax.dot_general(lhs, rhs, NT, preferred_element_type=jnp.float32)

    def tiles(body):
        @pl.loop(0, half // TILE)
        def _(j):
            here = pl.ds(pl.multiple_of(j * TILE, TILE), TILE)
            there = (j * TILE // share, pl.ds(pl.multiple_of(j * TILE % share, TILE), TILE))
            body(here, there)

    for copy in locals_:
        copy.wait()

    def project_query(here, there):
        total[:, here] = dot(dq_ref[...], mine[here, :feature])

    tiles(project_query)

    def project_query_far(here, there):
        total[:, here] += dot(dq_far[...], theirs[there[0], there[1], :feature])

    for t in range(planes):

        @pl.when(t <= z)
        def _(t=t):
            @pl.when(t == z)
            def _():
                query_swap.wait()
                weight_swap.wait()
                tiles(project_query_far)

            across(t).wait_recv()
            held[t] += y_in[t].astype(jnp.float32)

            @pl.when(z < planes - 1)
            def _():
                down(t).wait_recv()
                held[t] += z_in[t].astype(jnp.float32)

            @pl.when(t < z)
            def _():
                z_out[t] = held[t].astype(jnp.bfloat16)
                down(t).start()

            @pl.when(t == z)
            def _():
                dkv[:, :HD] = held[t, 0].astype(jnp.bfloat16)
                dkv[:, HD:] = held[t, 1].astype(jnp.bfloat16)

    keyval_swap.start()

    def project_keyval(here, there):
        total[:, here] += dot(dkv[...], mine[here, feature:])

    tiles(project_keyval)
    for t in range(planes):

        @pl.when(t <= z)
        def _(t=t):
            between(t).wait_send()
            across(t).wait_send()

            @pl.when(t < z)
            def _():
                down(t).wait_send()

    keyval_swap.wait()

    def project_keyval_far(here, there):
        out_ref[:, here] = (
            total[:, here] + dot(dkv_far[...], theirs[there[0], there[1], feature:])
        ).astype(jnp.bfloat16)

    tiles(project_keyval_far)


def close_blocks(part, dq, near, weights, planes):
    block = part.shape[3:]
    rows, width = dq.shape
    half = 2 * near.shape[0]
    dma = pltpu.SemaphoreType.DMA
    slots = pltpu.VMEM((planes,) + block, jnp.bfloat16)
    flat = pltpu.VMEM((rows, 2 * HD), jnp.bfloat16)
    vmem = pl.BlockSpec(memory_space=pltpu.VMEM)
    anywhere = pl.BlockSpec(memory_space=pl.ANY)
    return pl.pallas_call(
        functools.partial(close_kernel, planes),
        out_shape=jax.ShapeDtypeStruct((rows, half), jnp.bfloat16),
        in_specs=[vmem, vmem] + [anywhere] * 4,
        out_specs=vmem,
        scratch_shapes=[
            pltpu.VMEM((planes, 2) + block, jnp.bfloat16),
            slots, slots, slots, slots,
            pltpu.VMEM((planes,) + block, jnp.float32),
            pltpu.VMEM((half, near.shape[1]), jnp.bfloat16),
            pltpu.VMEM((2,) + near.shape, jnp.bfloat16),
            pltpu.VMEM(dq.shape, jnp.bfloat16),
            flat, flat,
            pltpu.VMEM((rows, half), jnp.float32),
        ] + [dma((planes,))] * 6 + [dma((4,)), dma(()), dma(()), dma((2,)), dma((2,))],
        compiler_params=pltpu.CompilerParams(
            collective_id=3, has_side_effects=True, vmem_limit_bytes=VMEM_LIMIT
        ),
        name="close_blocks",
    )(part, dq, near, *weights)


def on_device(
    queries, key_rows, value_rows, output_rows, output_grad, log_normalizer,
    selection, query_weight, key_weight, value_weight,
):
    position = lax.axis_index("ctx")
    contexts = lax.axis_size("ctx")
    groups = lax.axis_size("grp")
    planes = contexts // 4
    if groups == 2:
        weights = (query_weight, key_weight, value_weight)
        lse = log_normalizer.T
        blocks, near, dq, delta, known = open_blocks(
            key_rows, value_rows, queries, output_grad, output_rows, lse, weights, planes
        )
        grad_query, part = chosen_blocks(
            selection, queries, output_grad, lse, delta, dq, known, blocks
        )
        return close_blocks(part, grad_query, near, weights, planes)

    blocks = gather_blocks(jnp.concatenate([key_rows, value_rows], axis=1), planes)
    row = lax.dynamic_index_in_dim(selection, position, 0, keepdims=False).astype(jnp.int32)
    chosen = jnp.concatenate([position[None].astype(jnp.int32), row])
    usable = jnp.concatenate([jnp.ones((1,), jnp.int32), (row < position).astype(jnp.int32)])
    grad_query, part = attend(
        chosen, usable, queries, output_grad, output_rows, log_normalizer.T, blocks
    )
    grad_keyval = scatter_blocks(part, planes)
    dot = functools.partial(lax.dot_general, dimension_numbers=NT, preferred_element_type=jnp.float32)
    combined = dot(grad_query, query_weight)
    combined = combined + dot(grad_keyval[:, :HD], key_weight)
    combined = combined + dot(grad_keyval[:, HD:], value_weight)
    return lax.psum_scatter(combined.astype(jnp.bfloat16), "grp", scatter_dimension=1, tiled=True)


def solution(mesh):
    return jax.shard_map(
        on_device,
        mesh=mesh,
        in_specs=(
            P("ctx", "grp"),
            P("ctx", "grp"),
            P("ctx", "grp"),
            P("ctx", "grp"),
            P("ctx", "grp"),
            P("ctx", "grp"),
            P(),
            P(None, "grp"),
            P(None, "grp"),
            P(None, "grp"),
        ),
        out_specs=P("ctx", "grp"),
        check_vma=False,
    )
```

```python
import functools
import math

import jax
import jax.numpy as jnp
from jax import lax
from jax.experimental import pallas as pl
from jax.experimental.pallas import tpu as pltpu
from jax.sharding import PartitionSpec as P

HD = 128
BLOCK = 512
TOPK = 3
MESH = pl.DeviceIdType.MESH
SCALE = float(HD) ** (-0.5)
LOG2E = math.log2(math.e)
VMEM_LIMIT = 56 * 1024 * 1024
NT = (((1,), (1,)), ((), ()))
NN = (((1,), (0,)), ((), ()))


def place():
    me = lax.axis_index("ctx")
    return me, me // 4, (me // 2) % 2, me % 2


def sibling_of(me, core):
    return me + 1 - 2 * core


def beside(me, column):
    return me + 2 - 4 * column


def remote(src, dst, send, recv, target):
    return pltpu.make_async_remote_copy(
        src_ref=src, dst_ref=dst, send_sem=send, recv_sem=recv,
        device_id={"ctx": target}, device_id_type=MESH,
    )


def greet(target):
    pl.semaphore_signal(
        pltpu.get_barrier_semaphore(), inc=1, device_id={"ctx": target}, device_id_type=MESH
    )


def gather_kernel(planes, kv_ref, all_ref, own_sem, z_send, z_recv, y_send, y_recv, c_send, c_recv):
    me, z, y, c = place()
    sibling, side = sibling_of(me, c), beside(me, y)
    greet(sibling)
    greet(side)

    @pl.when(z > 0)
    def _():
        greet(me - 4)

    own = pltpu.make_async_copy(kv_ref, all_ref.at[z, c, y], own_sem)
    own.start()
    pl.semaphore_wait(pltpu.get_barrier_semaphore(), 2 + (z < planes - 1).astype(jnp.int32))

    def up(s):
        src = kv_ref if s == 0 else all_ref.at[z - s, c, y]
        return remote(src, all_ref.at[z - s, c, y], z_send.at[s], z_recv.at[s + 1], me + 4)

    def from_below(s):
        slot = all_ref.at[z - s, c, y]
        return remote(slot, slot, z_send.at[s], z_recv.at[s], me)

    def across(s):
        src = kv_ref if s == 0 else all_ref.at[z - s, c, y]
        return remote(src, all_ref.at[z - s, c, y], y_send.at[s], y_recv.at[s], side)

    def between(s):
        pair = all_ref.at[z - s, c]
        return remote(pair, pair, c_send.at[s], c_recv.at[s], sibling)

    for s in range(planes + 1):
        if s < planes:

            @pl.when(z >= s)
            def _(s=s):
                if s > 0:
                    from_below(s).wait_recv()
                if s < planes - 1:

                    @pl.when(z < planes - 1)
                    def _():
                        up(s).start()

                across(s).start()

        if s == 0:
            own.wait()
        else:

            @pl.when(z >= s - 1)
            def _(s=s):
                across(s - 1).wait_recv()
                between(s - 1).start()

    for s in range(planes):

        @pl.when(z >= s)
        def _(s=s):
            if s < planes - 1:

                @pl.when(z < planes - 1)
                def _():
                    up(s).wait_send()

            across(s).wait_send()
            between(s).wait()


def gather_blocks(kv, planes):
    shape = (planes, 2, 2) + kv.shape
    dma = pltpu.SemaphoreType.DMA
    return pl.pallas_call(
        functools.partial(gather_kernel, planes),
        out_shape=jax.ShapeDtypeStruct(shape, kv.dtype),
        in_specs=[pl.BlockSpec(memory_space=pl.ANY)],
        out_specs=pl.BlockSpec(memory_space=pl.ANY),
        scratch_shapes=[dma(())] + [dma((planes,))] * 6,
        compiler_params=pltpu.CompilerParams(collective_id=0, has_side_effects=True),
        name="gather_blocks",
    )(kv)


def attend_kernel(
    chosen_ref, usable_ref, q_ref, do_ref, o_ref, lse_ref, kv_ref,
    dq_ref, part_ref, delta, dq_sum,
):
    slot = pl.program_id(0)
    heads = q_ref.shape[1] // HD

    def columns(h):
        return slice(h * HD, (h + 1) * HD)

    @pl.when(slot == 0)
    def _():
        part_ref[...] = jnp.zeros_like(part_ref)
        dq_sum[...] = jnp.zeros_like(dq_sum)
        for h in range(heads):
            product = do_ref[:, columns(h)].astype(jnp.float32) * o_ref[:, columns(h)].astype(jnp.float32)
            delta[h : h + 1, :] = jnp.sum(product.T, axis=0, keepdims=True)

    def pair(diagonal):
        key = kv_ref[0, 0, 0, :, :HD]
        value = kv_ref[0, 0, 0, :, HD:]
        key_t = key.astype(jnp.float32).T.astype(jnp.bfloat16)
        if diagonal:
            key_pos = lax.broadcasted_iota(jnp.int32, (BLOCK, BLOCK), 0)
            query_pos = lax.broadcasted_iota(jnp.int32, (BLOCK, BLOCK), 1)
            seen = key_pos <= query_pos
        dk = jnp.zeros((BLOCK, HD), jnp.float32)
        dv = jnp.zeros((BLOCK, HD), jnp.float32)
        for h in range(heads):
            query, cotangent = q_ref[:, columns(h)], do_ref[:, columns(h)]
            scores = lax.dot_general(key, query, NT, preferred_element_type=jnp.float32)
            probs = jnp.exp2(scores * (SCALE * LOG2E) - lse_ref[h : h + 1, :] * LOG2E)
            if diagonal:
                probs = jnp.where(seen, probs, 0.0)
            prob_grad = lax.dot_general(value, cotangent, NT, preferred_element_type=jnp.float32)
            score_half = (probs * (prob_grad - delta[h : h + 1, :])).astype(jnp.bfloat16)
            probs_half = probs.astype(jnp.bfloat16)
            dv = dv + lax.dot_general(probs_half, cotangent, NN, preferred_element_type=jnp.float32)
            dk = dk + lax.dot_general(score_half, query, NN, preferred_element_type=jnp.float32)
            dq_sum[h] += lax.dot_general(key_t, score_half, NN, preferred_element_type=jnp.float32)
        block = chosen_ref[slot]
        at = (block // 4, block % 2, (block // 2) % 2)
        part_ref[at + (slice(None), slice(0, HD))] = (dk * SCALE).astype(jnp.bfloat16)
        part_ref[at + (slice(None), slice(HD, 2 * HD))] = dv.astype(jnp.bfloat16)

    @pl.when(slot == 0)
    def _():
        pair(True)

    @pl.when((slot > 0) & (usable_ref[slot] > 0))
    def _():
        pair(False)

    @pl.when(slot == TOPK)
    def _():
        for h in range(heads):
            dq_ref[:, columns(h)] = (dq_sum[h] * SCALE).T.astype(jnp.bfloat16)


def attend(chosen, usable, queries, output_grad, output_rows, lse, blocks):
    rows, width = queries.shape
    heads = width // HD
    whole = lambda s, chosen, usable: (0, 0)
    wide = pl.BlockSpec((rows, width), whole)
    return pl.pallas_call(
        attend_kernel,
        out_shape=(
            jax.ShapeDtypeStruct((rows, width), jnp.bfloat16),
            jax.ShapeDtypeStruct(blocks.shape, jnp.bfloat16),
        ),
        grid_spec=pltpu.PrefetchScalarGridSpec(
            num_scalar_prefetch=2,
            grid=(TOPK + 1,),
            in_specs=[
                wide, wide, wide,
                pl.BlockSpec((heads, rows), whole),
                pl.BlockSpec(
                    (1, 1, 1) + blocks.shape[3:],
                    lambda s, chosen, usable: (
                        chosen[s] // 4, chosen[s] % 2, (chosen[s] // 2) % 2, 0, 0,
                    ),
                ),
            ],
            out_specs=[wide, pl.BlockSpec(blocks.shape, lambda s, chosen, usable: (0,) * 5)],
            scratch_shapes=[
                pltpu.VMEM((heads, rows), jnp.float32),
                pltpu.VMEM((heads, HD, rows), jnp.float32),
            ],
        ),
        compiler_params=pltpu.CompilerParams(vmem_limit_bytes=VMEM_LIMIT),
        cost_estimate=pl.CostEstimate(flops=6 * 10**9, bytes_accessed=10 * 2**20, transcendentals=4 * 2**20),
        name="attend",
    )(chosen, usable, queries, output_grad, output_rows, lse, blocks)


def scatter_kernel(
    planes, part_ref, out_ref, c_in, y_in, z_in, y_out, z_out, held,
    z_send, z_recv, y_send, y_recv, c_send, c_recv,
):
    me, z, y, c = place()
    sibling, side = sibling_of(me, c), beside(me, y)
    greet(sibling)
    greet(side)

    @pl.when(z < planes - 1)
    def _():
        greet(me + 4)

    pl.semaphore_wait(pltpu.get_barrier_semaphore(), 2 + (z > 0).astype(jnp.int32))

    def between(t):
        return remote(part_ref.at[t, 1 - c], c_in.at[t], c_send.at[t], c_recv.at[t], sibling)

    def across(t):
        return remote(y_out.at[t], y_in.at[t], y_send.at[t], y_recv.at[t], side)

    def down(t):
        return remote(z_out.at[t], z_in.at[t], z_send.at[t], z_recv.at[t], me - 4)

    for t in range(planes):

        @pl.when(t <= z)
        def _(t=t):
            between(t).start()

    for t in range(planes):

        @pl.when(t <= z)
        def _(t=t):
            between(t).wait_recv()
            y_out[t] = (
                part_ref[t, c, 1 - y].astype(jnp.float32) + c_in[t, 1 - y].astype(jnp.float32)
            ).astype(jnp.bfloat16)
            across(t).start()
            held[t] = part_ref[t, c, y].astype(jnp.float32) + c_in[t, y].astype(jnp.float32)

    for t in range(planes):

        @pl.when(t <= z)
        def _(t=t):
            across(t).wait_recv()
            held[t] += y_in[t].astype(jnp.float32)

            @pl.when(z < planes - 1)
            def _():
                down(t).wait_recv()
                held[t] += z_in[t].astype(jnp.float32)

            @pl.when(t < z)
            def _():
                z_out[t] = held[t].astype(jnp.bfloat16)
                down(t).start()

            @pl.when(t == z)
            def _():
                out_ref[...] = held[t].astype(jnp.bfloat16)

    for t in range(planes):

        @pl.when(t <= z)
        def _(t=t):
            between(t).wait_send()
            across(t).wait_send()

            @pl.when(t < z)
            def _():
                down(t).wait_send()


def scatter_blocks(part, planes):
    block = part.shape[3:]
    dma = pltpu.SemaphoreType.DMA
    slots = pltpu.VMEM((planes,) + block, jnp.bfloat16)
    return pl.pallas_call(
        functools.partial(scatter_kernel, planes),
        out_shape=jax.ShapeDtypeStruct(block, jnp.bfloat16),
        in_specs=[pl.BlockSpec(memory_space=pltpu.VMEM)],
        out_specs=pl.BlockSpec(memory_space=pltpu.VMEM),
        scratch_shapes=[
            pltpu.VMEM((planes, 2) + block, jnp.bfloat16),
            slots, slots, slots, slots,
            pltpu.VMEM((planes,) + block, jnp.float32),
        ] + [dma((planes,))] * 6,
        compiler_params=pltpu.CompilerParams(
            collective_id=1, has_side_effects=True, vmem_limit_bytes=VMEM_LIMIT
        ),
        cost_estimate=pl.CostEstimate(flops=10**9, bytes_accessed=100 * 2**20, transcendentals=0),
        name="scatter_blocks",
    )(part)


def toward(src, dst, send, recv):
    return pltpu.make_async_remote_copy(
        src_ref=src, dst_ref=dst, send_sem=send, recv_sem=recv,
        device_id={"grp": 1 - lax.axis_index("grp")}, device_id_type=MESH,
    )


def greet_group():
    pl.semaphore_signal(
        pltpu.get_barrier_semaphore(), inc=1,
        device_id={"grp": 1 - lax.axis_index("grp")}, device_id_type=MESH,
    )


def columns(h):
    return slice(h * HD, (h + 1) * HD)


def block_gradients(key, value, q_ref, do_ref, lse_ref, delta_ref, dq_sum, diagonal):
    heads = q_ref.shape[1] // HD
    key_t = key.astype(jnp.float32).T.astype(jnp.bfloat16)
    if diagonal:
        key_pos = lax.broadcasted_iota(jnp.int32, (BLOCK, BLOCK), 0)
        query_pos = lax.broadcasted_iota(jnp.int32, (BLOCK, BLOCK), 1)
        seen = key_pos <= query_pos
    dk = jnp.zeros((BLOCK, HD), jnp.float32)
    dv = jnp.zeros((BLOCK, HD), jnp.float32)
    for h in range(heads):
        query, cotangent = q_ref[:, columns(h)], do_ref[:, columns(h)]
        scores = lax.dot_general(key, query, NT, preferred_element_type=jnp.float32)
        probs = jnp.exp2(scores * (SCALE * LOG2E) - lse_ref[h : h + 1, :] * LOG2E)
        if diagonal:
            probs = jnp.where(seen, probs, 0.0)
        prob_grad = lax.dot_general(value, cotangent, NT, preferred_element_type=jnp.float32)
        score_half = (probs * (prob_grad - delta_ref[h : h + 1, :])).astype(jnp.bfloat16)
        probs_half = probs.astype(jnp.bfloat16)
        dv = dv + lax.dot_general(probs_half, cotangent, NN, preferred_element_type=jnp.float32)
        dk = dk + lax.dot_general(score_half, query, NN, preferred_element_type=jnp.float32)
        dq = lax.dot_general(key_t, score_half, NN, preferred_element_type=jnp.float32)
        dq_sum[h] = dq if diagonal else dq_sum[h] + dq
    return (dk * SCALE).astype(jnp.bfloat16), dv.astype(jnp.bfloat16)


TILE = 256


def fused_kernel(
    planes, selection_ref, key_ref, value_ref, q_ref, do_ref, o_ref, lse_ref, wq_ref, wk_ref, wv_ref,
    out_ref,
    blocks, part, delta, dq_sum, picked, dq, dq_far, mine, theirs, total,
    c_in, y_in, z_in, y_out, z_out, held, dkv, dkv_far,
    gz_send, gz_recv, gy_send, gy_recv, gc_send, gc_recv,
    sz_send, sz_recv, sy_send, sy_recv, sc_send, sc_recv,
    local_sem, w_send, w_recv, swap_send, swap_recv, x_send, x_recv,
):
    me, z, y, c = place()
    group = lax.axis_index("grp")
    sibling, side = sibling_of(me, c), beside(me, y)
    heads = q_ref.shape[1] // HD
    feature = q_ref.shape[1]
    half = out_ref.shape[1]
    share = half // 2
    kinds = range(2)

    greet(sibling)
    greet(side)
    greet_group()

    @pl.when(z > 0)
    def _():
        greet(me - 4)

    @pl.when(z < planes - 1)
    def _():
        greet(me + 4)

    local_rows = pl.ds(pl.multiple_of(group * half, half), half)
    away_rows = pl.ds(pl.multiple_of((1 - group) * half + c * share, share), share)
    locals_, weights = [], []
    first = 0
    for i, weight in enumerate((wq_ref, wk_ref, wv_ref)):
        last = first + weight.shape[1]
        locals_.append(
            pltpu.make_async_copy(weight.at[local_rows], mine.at[:, first:last], local_sem.at[i])
        )
        weights.append(
            toward(weight.at[away_rows], theirs.at[c, :, first:last], w_send.at[i], w_recv.at[i])
        )
        first = last
    weight_swap = remote(theirs.at[c], theirs.at[c], swap_send, swap_recv, sibling)

    blocks[z, c, 0, y] = key_ref[...]
    blocks[z, c, 1, y] = value_ref[...]
    pl.semaphore_wait(
        pltpu.get_barrier_semaphore(),
        3 + (z > 0).astype(jnp.int32) + (z < planes - 1).astype(jnp.int32),
    )

    def up(s, k):
        slot = blocks.at[z - s, c, k, y]
        return remote(slot, slot, gz_send.at[s, k], gz_recv.at[s + 1, k], me + 4)

    def from_below(s, k):
        slot = blocks.at[z - s, c, k, y]
        return remote(slot, slot, gz_send.at[s, k], gz_recv.at[s, k], me)

    def across(s, k):
        slot = blocks.at[z - s, c, k, y]
        return remote(slot, slot, gy_send.at[s, k], gy_recv.at[s, k], side)

    def between(s, k):
        pair = blocks.at[z - s, c, k]
        return remote(pair, pair, gc_send.at[s, k], gc_recv.at[s, k], sibling)

    def gradients(key, value, diagonal):
        return block_gradients(key, value, q_ref, do_ref, lse_ref, delta, dq_sum, diagonal)

    for s in range(planes + 1):
        for k in kinds:
            if s < planes:

                @pl.when(z >= s)
                def _(s=s, k=k):
                    if s > 0:
                        from_below(s, k).wait_recv()
                    if s < planes - 1:

                        @pl.when(z < planes - 1)
                        def _():
                            up(s, k).start()

                    across(s, k).start()

            if s > 0:

                @pl.when(z >= s - 1)
                def _(s=s, k=k):
                    across(s - 1, k).wait_recv()
                    between(s - 1, k).start()

        if s == 0:
            for copy in weights + locals_:
                copy.start()
            for h in range(heads):
                product = do_ref[:, columns(h)].astype(jnp.float32) * o_ref[:, columns(h)].astype(jnp.float32)
                delta[h : h + 1, :] = jnp.sum(product.T, axis=0, keepdims=True)
            dk, dv = gradients(key_ref[...], value_ref[...], True)
            picked[0, 0] = dk
            picked[0, 1] = dv

        if s == 2:
            for k in kinds:
                between(0, k).wait_recv()

                @pl.when(z >= 1)
                def _(k=k):
                    between(1, k).wait_recv()

            @pl.when(me > 0)
            def _():
                last = me - 1
                dk, dv = gradients(
                    blocks[last // 4, last % 2, 0, (last // 2) % 2],
                    blocks[last // 4, last % 2, 1, (last // 2) % 2],
                    False,
                )
                picked[1, 0] = dk
                picked[1, 1] = dv

    for s in range(2, planes):

        @pl.when(z >= s)
        def _(s=s):
            for k in kinds:
                between(s, k).wait_recv()

    picks = [selection_ref[me, column] for column in range(TOPK)]
    others = [
        jnp.where(picks[0] == me - 1, picks[1], picks[0]),
        jnp.where(picks[2] == me - 1, picks[1], picks[2]),
    ]
    for i, block in enumerate(others):
        usable = block < me
        at = jnp.where(usable, block, me)
        for h in range(heads):
            dq_sum[heads + h] = dq_sum[h]
        dk, dv = gradients(
            blocks[at // 4, at % 2, 0, (at // 2) % 2], blocks[at // 4, at % 2, 1, (at // 2) % 2], False
        )
        for h in range(heads):
            dq_sum[h] = jnp.where(usable, dq_sum[h], dq_sum[heads + h])
        picked[2 + i, 0] = dk
        picked[2 + i, 1] = dv
    for h in range(heads):
        dq[:, columns(h)] = (dq_sum[h] * SCALE).T.astype(jnp.bfloat16)
    query_swap = toward(dq, dq_far, x_send.at[2], x_recv.at[2])
    query_swap.start()

    def inward(t, k):
        return remote(part.at[t, 1 - c, k], c_in.at[t, k], sc_send.at[t, k], sc_recv.at[t, k], sibling)

    def sideways(t, k):
        return remote(y_out.at[t, k], y_in.at[t, k], sy_send.at[t, k], sy_recv.at[t, k], side)

    def down(t, k):
        return remote(z_out.at[t, k], z_in.at[t, k], sz_send.at[t, k], sz_recv.at[t, k], me - 4)

    def keyval_swap(k):
        return toward(dkv.at[k], dkv_far.at[k], x_send.at[k], x_recv.at[k])

    def place_partials(t, core):
        for column in range(2):
            block = t * 4 + column * 2 + core
            for k in kinds:
                nothing = jnp.zeros((BLOCK, HD), jnp.bfloat16)
                chosen = jnp.where((others[0] == block) & (block < me), picked[2, k], nothing)
                chosen = jnp.where((others[1] == block) & (block < me), picked[3, k], chosen)
                part[t, core, k, column] = chosen

                @pl.when(block == me)
                def _(k=k, column=column):
                    part[t, core, k, column] = picked[0, k]

                @pl.when(block == me - 1)
                def _(k=k, column=column):
                    part[t, core, k, column] = picked[1, k]

    for t in range(planes):

        @pl.when(t <= z)
        def _(t=t):
            place_partials(t, 1 - c)
            for k in kinds:
                inward(t, k).start()

    for t in range(planes):

        @pl.when(t <= z)
        def _(t=t):
            place_partials(t, c)
            for k in kinds:
                inward(t, k).wait_recv()
                y_out[t, k] = (
                    part[t, c, k, 1 - y].astype(jnp.float32) + c_in[t, k, 1 - y].astype(jnp.float32)
                ).astype(jnp.bfloat16)
                sideways(t, k).start()
                held[t, k] = part[t, c, k, y].astype(jnp.float32) + c_in[t, k, y].astype(jnp.float32)

    def dot(lhs, rhs):
        return lax.dot_general(lhs, rhs, NT, preferred_element_type=jnp.float32)

    def tiles(body):
        @pl.loop(0, half // TILE)
        def _(j):
            here = pl.ds(pl.multiple_of(j * TILE, TILE), TILE)
            there = (j * TILE // share, pl.ds(pl.multiple_of(j * TILE % share, TILE), TILE))
            body(here, there)

    for copy in locals_:
        copy.wait()

    def project_query(here, there):
        total[:, here] = dot(dq[...], mine[here, :feature])

    tiles(project_query)
    for copy in weights:
        copy.wait_recv()
    weight_swap.start()

    def project_query_far(here, there):
        total[:, here] += dot(dq_far[...], theirs[there[0], there[1], :feature])

    for t in range(planes):

        @pl.when(t <= z)
        def _(t=t):
            @pl.when(t == z)
            def _():
                query_swap.wait()
                weight_swap.wait()
                tiles(project_query_far)

            for k in kinds:
                sideways(t, k).wait_recv()
                held[t, k] += y_in[t, k].astype(jnp.float32)

                @pl.when(z < planes - 1)
                def _(k=k):
                    down(t, k).wait_recv()
                    held[t, k] += z_in[t, k].astype(jnp.float32)

                @pl.when(t < z)
                def _(k=k):
                    z_out[t, k] = held[t, k].astype(jnp.bfloat16)
                    down(t, k).start()

                @pl.when(t == z)
                def _(k=k):
                    dkv[k] = held[t, k].astype(jnp.bfloat16)
                    keyval_swap(k).start()

    def project_keyval(here, there):
        total[:, here] += dot(dkv[0], mine[here, feature : feature + HD]) + dot(
            dkv[1], mine[here, feature + HD :]
        )

    tiles(project_keyval)
    for s in range(planes):

        @pl.when(z >= s)
        def _(s=s):
            for k in kinds:
                if s < planes - 1:

                    @pl.when(z < planes - 1)
                    def _(k=k):
                        up(s, k).wait_send()

                across(s, k).wait_send()
                between(s, k).wait_send()
                inward(s, k).wait_send()
                sideways(s, k).wait_send()

                @pl.when(s < z)
                def _(k=k):
                    down(s, k).wait_send()

    for copy in weights:
        copy.wait_send()
    for k in kinds:
        keyval_swap(k).wait()

    def project_keyval_far(here, there):
        out_ref[:, here] = (
            total[:, here]
            + dot(dkv_far[0], theirs[there[0], there[1], feature : feature + HD])
            + dot(dkv_far[1], theirs[there[0], there[1], feature + HD :])
        ).astype(jnp.bfloat16)

    tiles(project_keyval_far)


def fused(selection, key, value, queries, output_grad, output_rows, lse, weights, planes):
    rows, width = queries.shape
    heads = width // HD
    half = weights[0].shape[0] // 2
    features = sum(weight.shape[1] for weight in weights)
    dma = pltpu.SemaphoreType.DMA
    vmem = pl.BlockSpec(memory_space=pltpu.VMEM)
    anywhere = pl.BlockSpec(memory_space=pl.ANY)

    def half_type(*shape):
        return pltpu.VMEM(shape, jnp.bfloat16)

    def full_type(*shape):
        return pltpu.VMEM(shape, jnp.float32)

    slots = half_type(planes, 2, rows, HD)
    return pl.pallas_call(
        functools.partial(fused_kernel, planes),
        out_shape=jax.ShapeDtypeStruct((rows, half), jnp.bfloat16),
        in_specs=[pl.BlockSpec(memory_space=pltpu.SMEM)] + [vmem] * 6 + [anywhere] * 3,
        out_specs=vmem,
        scratch_shapes=[
            half_type(planes, 2, 2, 2, rows, HD),
            half_type(planes, 2, 2, 2, rows, HD),
            full_type(heads, rows),
            full_type(2 * heads, HD, rows),
            half_type(4, 2, rows, HD),
            half_type(rows, width),
            half_type(rows, width),
            half_type(half, features),
            half_type(2, half // 2, features),
            full_type(rows, half),
            half_type(planes, 2, 2, rows, HD),
            slots, slots, slots, slots,
            full_type(planes, 2, rows, HD),
            half_type(2, rows, HD),
            half_type(2, rows, HD),
        ] + [dma((planes, 2))] * 12 + [dma((3,)), dma((3,)), dma((3,)), dma(()), dma(()), dma((3,)), dma((3,))],
        compiler_params=pltpu.CompilerParams(
            collective_id=2, has_side_effects=True, vmem_limit_bytes=VMEM_LIMIT
        ),
        name="fused",
    )(selection, key, value, queries, output_grad, output_rows, lse, *weights)


def on_device(
    queries, key_rows, value_rows, output_rows, output_grad, log_normalizer,
    selection, query_weight, key_weight, value_weight,
):
    position = lax.axis_index("ctx")
    contexts = lax.axis_size("ctx")
    groups = lax.axis_size("grp")
    planes = contexts // 4
    if groups == 2:
        weights = (query_weight, key_weight, value_weight)
        lse = log_normalizer.T
        return fused(
            selection, key_rows, value_rows, queries, output_grad, output_rows, lse, weights, planes
        )

    blocks = gather_blocks(jnp.concatenate([key_rows, value_rows], axis=1), planes)
    row = lax.dynamic_index_in_dim(selection, position, 0, keepdims=False).astype(jnp.int32)
    chosen = jnp.concatenate([position[None].astype(jnp.int32), row])
    usable = jnp.concatenate([jnp.ones((1,), jnp.int32), (row < position).astype(jnp.int32)])
    grad_query, part = attend(
        chosen, usable, queries, output_grad, output_rows, log_normalizer.T, blocks
    )
    grad_keyval = scatter_blocks(part, planes)
    dot = functools.partial(lax.dot_general, dimension_numbers=NT, preferred_element_type=jnp.float32)
    combined = dot(grad_query, query_weight)
    combined = combined + dot(grad_keyval[:, :HD], key_weight)
    combined = combined + dot(grad_keyval[:, HD:], value_weight)
    return lax.psum_scatter(combined.astype(jnp.bfloat16), "grp", scatter_dimension=1, tiled=True)


def solution(mesh):
    return jax.shard_map(
        on_device,
        mesh=mesh,
        in_specs=(
            P("ctx", "grp"),
            P("ctx", "grp"),
            P("ctx", "grp"),
            P("ctx", "grp"),
            P("ctx", "grp"),
            P("ctx", "grp"),
            P(),
            P(None, "grp"),
            P(None, "grp"),
            P(None, "grp"),
        ),
        out_specs=P("ctx", "grp"),
        check_vma=False,
    )
```

```python
import functools
import math

import jax
import jax.numpy as jnp
from jax import lax
from jax.experimental import pallas as pl
from jax.experimental.pallas import tpu as pltpu
from jax.sharding import PartitionSpec as P

HD = 128
BLOCK = 512
TOPK = 3
MESH = pl.DeviceIdType.MESH
SCALE = float(HD) ** (-0.5)
LOG2E = math.log2(math.e)
VMEM_LIMIT = 56 * 1024 * 1024
NT = (((1,), (1,)), ((), ()))
NN = (((1,), (0,)), ((), ()))


def place():
    me = lax.axis_index("ctx")
    return me, me // 4, (me // 2) % 2, me % 2


def sibling_of(me, core):
    return me + 1 - 2 * core


def beside(me, column):
    return me + 2 - 4 * column


def remote(src, dst, send, recv, target):
    return pltpu.make_async_remote_copy(
        src_ref=src, dst_ref=dst, send_sem=send, recv_sem=recv,
        device_id={"ctx": target}, device_id_type=MESH,
    )


def greet(target):
    pl.semaphore_signal(
        pltpu.get_barrier_semaphore(), inc=1, device_id={"ctx": target}, device_id_type=MESH
    )


def gather_kernel(planes, kv_ref, all_ref, own_sem, z_send, z_recv, y_send, y_recv, c_send, c_recv):
    me, z, y, c = place()
    sibling, side = sibling_of(me, c), beside(me, y)
    greet(sibling)
    greet(side)

    @pl.when(z > 0)
    def _():
        greet(me - 4)

    own = pltpu.make_async_copy(kv_ref, all_ref.at[z, c, y], own_sem)
    own.start()
    pl.semaphore_wait(pltpu.get_barrier_semaphore(), 2 + (z < planes - 1).astype(jnp.int32))

    def up(s):
        src = kv_ref if s == 0 else all_ref.at[z - s, c, y]
        return remote(src, all_ref.at[z - s, c, y], z_send.at[s], z_recv.at[s + 1], me + 4)

    def from_below(s):
        slot = all_ref.at[z - s, c, y]
        return remote(slot, slot, z_send.at[s], z_recv.at[s], me)

    def across(s):
        src = kv_ref if s == 0 else all_ref.at[z - s, c, y]
        return remote(src, all_ref.at[z - s, c, y], y_send.at[s], y_recv.at[s], side)

    def between(s):
        pair = all_ref.at[z - s, c]
        return remote(pair, pair, c_send.at[s], c_recv.at[s], sibling)

    for s in range(planes + 1):
        if s < planes:

            @pl.when(z >= s)
            def _(s=s):
                if s > 0:
                    from_below(s).wait_recv()
                if s < planes - 1:

                    @pl.when(z < planes - 1)
                    def _():
                        up(s).start()

                across(s).start()

        if s == 0:
            own.wait()
        else:

            @pl.when(z >= s - 1)
            def _(s=s):
                across(s - 1).wait_recv()
                between(s - 1).start()

    for s in range(planes):

        @pl.when(z >= s)
        def _(s=s):
            if s < planes - 1:

                @pl.when(z < planes - 1)
                def _():
                    up(s).wait_send()

            across(s).wait_send()
            between(s).wait()


def gather_blocks(kv, planes):
    shape = (planes, 2, 2) + kv.shape
    dma = pltpu.SemaphoreType.DMA
    return pl.pallas_call(
        functools.partial(gather_kernel, planes),
        out_shape=jax.ShapeDtypeStruct(shape, kv.dtype),
        in_specs=[pl.BlockSpec(memory_space=pl.ANY)],
        out_specs=pl.BlockSpec(memory_space=pl.ANY),
        scratch_shapes=[dma(())] + [dma((planes,))] * 6,
        compiler_params=pltpu.CompilerParams(collective_id=0, has_side_effects=True),
        name="gather_blocks",
    )(kv)


def attend_kernel(
    chosen_ref, usable_ref, q_ref, do_ref, o_ref, lse_ref, kv_ref,
    dq_ref, part_ref, delta, dq_sum,
):
    slot = pl.program_id(0)
    heads = q_ref.shape[1] // HD

    def columns(h):
        return slice(h * HD, (h + 1) * HD)

    @pl.when(slot == 0)
    def _():
        part_ref[...] = jnp.zeros_like(part_ref)
        dq_sum[...] = jnp.zeros_like(dq_sum)
        for h in range(heads):
            product = do_ref[:, columns(h)].astype(jnp.float32) * o_ref[:, columns(h)].astype(jnp.float32)
            delta[h : h + 1, :] = jnp.sum(product.T, axis=0, keepdims=True)

    def pair(diagonal):
        key = kv_ref[0, 0, 0, :, :HD]
        value = kv_ref[0, 0, 0, :, HD:]
        key_t = key.astype(jnp.float32).T.astype(jnp.bfloat16)
        if diagonal:
            key_pos = lax.broadcasted_iota(jnp.int32, (BLOCK, BLOCK), 0)
            query_pos = lax.broadcasted_iota(jnp.int32, (BLOCK, BLOCK), 1)
            seen = key_pos <= query_pos
        dk = jnp.zeros((BLOCK, HD), jnp.float32)
        dv = jnp.zeros((BLOCK, HD), jnp.float32)
        for h in range(heads):
            query, cotangent = q_ref[:, columns(h)], do_ref[:, columns(h)]
            scores = lax.dot_general(key, query, NT, preferred_element_type=jnp.float32)
            probs = jnp.exp2(scores * (SCALE * LOG2E) - lse_ref[h : h + 1, :] * LOG2E)
            if diagonal:
                probs = jnp.where(seen, probs, 0.0)
            prob_grad = lax.dot_general(value, cotangent, NT, preferred_element_type=jnp.float32)
            score_half = (probs * (prob_grad - delta[h : h + 1, :])).astype(jnp.bfloat16)
            probs_half = probs.astype(jnp.bfloat16)
            dv = dv + lax.dot_general(probs_half, cotangent, NN, preferred_element_type=jnp.float32)
            dk = dk + lax.dot_general(score_half, query, NN, preferred_element_type=jnp.float32)
            dq_sum[h] += lax.dot_general(key_t, score_half, NN, preferred_element_type=jnp.float32)
        block = chosen_ref[slot]
        at = (block // 4, block % 2, (block // 2) % 2)
        part_ref[at + (slice(None), slice(0, HD))] = (dk * SCALE).astype(jnp.bfloat16)
        part_ref[at + (slice(None), slice(HD, 2 * HD))] = dv.astype(jnp.bfloat16)

    @pl.when(slot == 0)
    def _():
        pair(True)

    @pl.when((slot > 0) & (usable_ref[slot] > 0))
    def _():
        pair(False)

    @pl.when(slot == TOPK)
    def _():
        for h in range(heads):
            dq_ref[:, columns(h)] = (dq_sum[h] * SCALE).T.astype(jnp.bfloat16)


def attend(chosen, usable, queries, output_grad, output_rows, lse, blocks):
    rows, width = queries.shape
    heads = width // HD
    whole = lambda s, chosen, usable: (0, 0)
    wide = pl.BlockSpec((rows, width), whole)
    return pl.pallas_call(
        attend_kernel,
        out_shape=(
            jax.ShapeDtypeStruct((rows, width), jnp.bfloat16),
            jax.ShapeDtypeStruct(blocks.shape, jnp.bfloat16),
        ),
        grid_spec=pltpu.PrefetchScalarGridSpec(
            num_scalar_prefetch=2,
            grid=(TOPK + 1,),
            in_specs=[
                wide, wide, wide,
                pl.BlockSpec((heads, rows), whole),
                pl.BlockSpec(
                    (1, 1, 1) + blocks.shape[3:],
                    lambda s, chosen, usable: (
                        chosen[s] // 4, chosen[s] % 2, (chosen[s] // 2) % 2, 0, 0,
                    ),
                ),
            ],
            out_specs=[wide, pl.BlockSpec(blocks.shape, lambda s, chosen, usable: (0,) * 5)],
            scratch_shapes=[
                pltpu.VMEM((heads, rows), jnp.float32),
                pltpu.VMEM((heads, HD, rows), jnp.float32),
            ],
        ),
        compiler_params=pltpu.CompilerParams(vmem_limit_bytes=VMEM_LIMIT),
        cost_estimate=pl.CostEstimate(flops=6 * 10**9, bytes_accessed=10 * 2**20, transcendentals=4 * 2**20),
        name="attend",
    )(chosen, usable, queries, output_grad, output_rows, lse, blocks)


def scatter_kernel(
    planes, part_ref, out_ref, c_in, y_in, z_in, y_out, z_out, held,
    z_send, z_recv, y_send, y_recv, c_send, c_recv,
):
    me, z, y, c = place()
    sibling, side = sibling_of(me, c), beside(me, y)
    greet(sibling)
    greet(side)

    @pl.when(z < planes - 1)
    def _():
        greet(me + 4)

    pl.semaphore_wait(pltpu.get_barrier_semaphore(), 2 + (z > 0).astype(jnp.int32))

    def between(t):
        return remote(part_ref.at[t, 1 - c], c_in.at[t], c_send.at[t], c_recv.at[t], sibling)

    def across(t):
        return remote(y_out.at[t], y_in.at[t], y_send.at[t], y_recv.at[t], side)

    def down(t):
        return remote(z_out.at[t], z_in.at[t], z_send.at[t], z_recv.at[t], me - 4)

    for t in range(planes):

        @pl.when(t <= z)
        def _(t=t):
            between(t).start()

    for t in range(planes):

        @pl.when(t <= z)
        def _(t=t):
            between(t).wait_recv()
            y_out[t] = (
                part_ref[t, c, 1 - y].astype(jnp.float32) + c_in[t, 1 - y].astype(jnp.float32)
            ).astype(jnp.bfloat16)
            across(t).start()
            held[t] = part_ref[t, c, y].astype(jnp.float32) + c_in[t, y].astype(jnp.float32)

    for t in range(planes):

        @pl.when(t <= z)
        def _(t=t):
            across(t).wait_recv()
            held[t] += y_in[t].astype(jnp.float32)

            @pl.when(z < planes - 1)
            def _():
                down(t).wait_recv()
                held[t] += z_in[t].astype(jnp.float32)

            @pl.when(t < z)
            def _():
                z_out[t] = held[t].astype(jnp.bfloat16)
                down(t).start()

            @pl.when(t == z)
            def _():
                out_ref[...] = held[t].astype(jnp.bfloat16)

    for t in range(planes):

        @pl.when(t <= z)
        def _(t=t):
            between(t).wait_send()
            across(t).wait_send()

            @pl.when(t < z)
            def _():
                down(t).wait_send()


def scatter_blocks(part, planes):
    block = part.shape[3:]
    dma = pltpu.SemaphoreType.DMA
    slots = pltpu.VMEM((planes,) + block, jnp.bfloat16)
    return pl.pallas_call(
        functools.partial(scatter_kernel, planes),
        out_shape=jax.ShapeDtypeStruct(block, jnp.bfloat16),
        in_specs=[pl.BlockSpec(memory_space=pltpu.VMEM)],
        out_specs=pl.BlockSpec(memory_space=pltpu.VMEM),
        scratch_shapes=[
            pltpu.VMEM((planes, 2) + block, jnp.bfloat16),
            slots, slots, slots, slots,
            pltpu.VMEM((planes,) + block, jnp.float32),
        ] + [dma((planes,))] * 6,
        compiler_params=pltpu.CompilerParams(
            collective_id=1, has_side_effects=True, vmem_limit_bytes=VMEM_LIMIT
        ),
        cost_estimate=pl.CostEstimate(flops=10**9, bytes_accessed=100 * 2**20, transcendentals=0),
        name="scatter_blocks",
    )(part)


def toward(src, dst, send, recv):
    return pltpu.make_async_remote_copy(
        src_ref=src, dst_ref=dst, send_sem=send, recv_sem=recv,
        device_id={"grp": 1 - lax.axis_index("grp")}, device_id_type=MESH,
    )


def greet_group():
    pl.semaphore_signal(
        pltpu.get_barrier_semaphore(), inc=1,
        device_id={"grp": 1 - lax.axis_index("grp")}, device_id_type=MESH,
    )


def columns(h):
    return slice(h * HD, (h + 1) * HD)


def block_gradients(key, value, q_ref, do_ref, lse_ref, delta_ref, dq_sum, diagonal):
    heads = q_ref.shape[1] // HD
    key_t = key.astype(jnp.float32).T.astype(jnp.bfloat16)
    if diagonal:
        key_pos = lax.broadcasted_iota(jnp.int32, (BLOCK, BLOCK), 0)
        query_pos = lax.broadcasted_iota(jnp.int32, (BLOCK, BLOCK), 1)
        seen = key_pos <= query_pos
    dk = jnp.zeros((BLOCK, HD), jnp.float32)
    dv = jnp.zeros((BLOCK, HD), jnp.float32)
    for h in range(heads):
        query, cotangent = q_ref[:, columns(h)], do_ref[:, columns(h)]
        scores = lax.dot_general(key, query, NT, preferred_element_type=jnp.float32)
        probs = jnp.exp2(scores * (SCALE * LOG2E) - lse_ref[h : h + 1, :] * LOG2E)
        if diagonal:
            probs = jnp.where(seen, probs, 0.0)
        prob_grad = lax.dot_general(value, cotangent, NT, preferred_element_type=jnp.float32)
        score_half = (probs * (prob_grad - delta_ref[h : h + 1, :])).astype(jnp.bfloat16)
        probs_half = probs.astype(jnp.bfloat16)
        dv = dv + lax.dot_general(probs_half, cotangent, NN, preferred_element_type=jnp.float32)
        dk = dk + lax.dot_general(score_half, query, NN, preferred_element_type=jnp.float32)
        dq = lax.dot_general(key_t, score_half, NN, preferred_element_type=jnp.float32)
        dq_sum[h] = dq if diagonal else dq_sum[h] + dq
    return (dk * SCALE).astype(jnp.bfloat16), dv.astype(jnp.bfloat16)


TILE = 256


def fused_kernel(
    planes, selection_ref, key_ref, value_ref, q_ref, do_ref, o_ref, lse_ref, wq_ref, wk_ref, wv_ref,
    out_ref, dkv_far, far_ref,
    blocks, part, delta, dq_sum, picked, dq, dq_far, mine, theirs, total,
    c_in, y_in, z_in, y_out, z_out, held, dkv, summed, extra_in,
    gz_send, gz_recv, gy_send, gy_recv, gc_send, gc_recv,
    sz_send, sz_recv, sy_send, sy_recv, sc_send, sc_recv,
    local_sem, w_send, w_recv, swap_send, swap_recv, x_send, x_recv,
    extra_send, extra_recv, write_sem,
):
    me, z, y, c = place()
    group = lax.axis_index("grp")
    sibling, side = sibling_of(me, c), beside(me, y)
    heads = q_ref.shape[1] // HD
    feature = q_ref.shape[1]
    half = out_ref.shape[1]
    share = half // 2
    kinds = range(2)

    greet(sibling)
    greet(side)
    greet_group()

    @pl.when(z > 0)
    def _():
        greet(me - 4)

    @pl.when(z < planes - 1)
    def _():
        greet(me + 4)

    local_rows = pl.ds(pl.multiple_of(group * half, half), half)
    away_rows = pl.ds(pl.multiple_of((1 - group) * half + c * share, share), share)
    locals_, weights = [], []
    first = 0
    for i, weight in enumerate((wq_ref, wk_ref, wv_ref)):
        last = first + weight.shape[1]
        locals_.append(
            pltpu.make_async_copy(weight.at[local_rows], mine.at[:, first:last], local_sem.at[i])
        )
        weights.append(
            toward(weight.at[away_rows], theirs.at[c, :, first:last], w_send.at[i], w_recv.at[i])
        )
        first = last
    weight_swap = remote(theirs.at[c], theirs.at[c], swap_send, swap_recv, sibling)

    blocks[z, c, 0, y] = key_ref[...]
    blocks[z, c, 1, y] = value_ref[...]
    pl.semaphore_wait(
        pltpu.get_barrier_semaphore(),
        3 + (z > 0).astype(jnp.int32) + (z < planes - 1).astype(jnp.int32),
    )

    def up(s, k):
        slot = blocks.at[z - s, c, k, y]
        return remote(slot, slot, gz_send.at[s, k], gz_recv.at[s + 1, k], me + 4)

    def from_below(s, k):
        slot = blocks.at[z - s, c, k, y]
        return remote(slot, slot, gz_send.at[s, k], gz_recv.at[s, k], me)

    def across(s, k):
        slot = blocks.at[z - s, c, k, y]
        return remote(slot, slot, gy_send.at[s, k], gy_recv.at[s, k], side)

    def between(s, k):
        pair = blocks.at[z - s, c, k]
        return remote(pair, pair, gc_send.at[s, k], gc_recv.at[s, k], sibling)

    def extra_up():
        slot = blocks.at[0, c, 1, 1 - y]
        return remote(slot, slot, extra_send.at[0], extra_recv.at[0], me + 4)

    def gradients(key, value, diagonal):
        return block_gradients(key, value, q_ref, do_ref, lse_ref, delta, dq_sum, diagonal)

    for s in range(planes + 1):
        for k in kinds:
            if s < planes:

                @pl.when(z >= s)
                def _(s=s, k=k):
                    if s > 0:
                        from_below(s, k).wait_recv()
                    if s < planes - 1:

                        @pl.when(z < planes - 1)
                        def _():
                            up(s, k).start()

                    if (s, k) != (planes - 1, 1):
                        across(s, k).start()

            if s > 0:

                @pl.when(z >= s - 1)
                def _(s=s, k=k):
                    if (s, k) != (planes, 1):
                        across(s - 1, k).wait_recv()
                    else:
                        extra_up().wait_recv()
                    if (s, k) == (planes - 1, 1):

                        @pl.when(z == planes - 2)
                        def _():
                            extra_up().start()

                    between(s - 1, k).start()

        if s == 0:
            for copy in weights + locals_:
                copy.start()
            for h in range(heads):
                product = do_ref[:, columns(h)].astype(jnp.float32) * o_ref[:, columns(h)].astype(jnp.float32)
                delta[h : h + 1, :] = jnp.sum(product.T, axis=0, keepdims=True)
            dk, dv = gradients(key_ref[...], value_ref[...], True)
            picked[0, 0] = dk
            picked[0, 1] = dv

        if s == 2:
            for k in kinds:
                between(0, k).wait_recv()

                @pl.when(z >= 1)
                def _(k=k):
                    between(1, k).wait_recv()

            @pl.when(me > 0)
            def _():
                last = me - 1
                dk, dv = gradients(
                    blocks[last // 4, last % 2, 0, (last // 2) % 2],
                    blocks[last // 4, last % 2, 1, (last // 2) % 2],
                    False,
                )
                picked[1, 0] = dk
                picked[1, 1] = dv

    for s in range(2, planes):

        @pl.when(z >= s)
        def _(s=s):
            for k in kinds:
                between(s, k).wait_recv()

    picks = [selection_ref[column, me] for column in range(TOPK)]
    others = [
        jnp.where(picks[0] == me - 1, picks[1], picks[0]),
        jnp.where(picks[2] == me - 1, picks[1], picks[2]),
    ]
    for i, block in enumerate(others):
        usable = block < me
        at = jnp.where(usable, block, me)
        for h in range(heads):
            dq_sum[heads + h] = dq_sum[h]
        dk, dv = gradients(
            blocks[at // 4, at % 2, 0, (at // 2) % 2], blocks[at // 4, at % 2, 1, (at // 2) % 2], False
        )
        for h in range(heads):
            dq_sum[h] = jnp.where(usable, dq_sum[h], dq_sum[heads + h])
        picked[2 + i, 0] = dk
        picked[2 + i, 1] = dv
    for h in range(heads):
        dq[:, columns(h)] = (dq_sum[h] * SCALE).T.astype(jnp.bfloat16)
    query_swap = toward(dq, dq_far, x_send.at[2], x_recv.at[2])
    query_swap.start()

    def inward(t, k):
        return remote(part.at[t, 1 - c, k], c_in.at[t, k], sc_send.at[t, k], sc_recv.at[t, k], sibling)

    def sideways(t, k):
        return remote(y_out.at[t, k], y_in.at[t, k], sy_send.at[t, k], sy_recv.at[t, k], side)

    def down(t, k):
        return remote(z_out.at[t, k], z_in.at[t, k], sz_send.at[t, k], sz_recv.at[t, k], me - 4)

    def extra_down():
        return remote(y_out.at[0, 0], extra_in, extra_send.at[1], extra_recv.at[1], me - 4)

    def keyval_swap(k):
        return toward(dkv.at[k], dkv_far.at[k], x_send.at[k], x_recv.at[k])

    def place_partials(t, core):
        for column in range(2):
            block = t * 4 + column * 2 + core
            for k in kinds:
                nothing = jnp.zeros((BLOCK, HD), jnp.bfloat16)
                chosen = jnp.where((others[0] == block) & (block < me), picked[2, k], nothing)
                chosen = jnp.where((others[1] == block) & (block < me), picked[3, k], chosen)
                part[t, core, k, column] = chosen

                @pl.when(block == me)
                def _(k=k, column=column):
                    part[t, core, k, column] = picked[0, k]

                @pl.when(block == me - 1)
                def _(k=k, column=column):
                    part[t, core, k, column] = picked[1, k]

    for t in range(planes):

        @pl.when(t <= z)
        def _(t=t):
            place_partials(t, 1 - c)
            for k in kinds:
                inward(t, k).start()

    for t in range(planes):

        @pl.when(t <= z)
        def _(t=t):
            place_partials(t, c)
            for k in (1, 0) if t == 0 else (0, 1):
                inward(t, k).wait_recv()
                away = part[t, c, k, 1 - y].astype(jnp.float32) + c_in[t, k, 1 - y].astype(jnp.float32)
                held[t, k] = part[t, c, k, y].astype(jnp.float32) + c_in[t, k, y].astype(jnp.float32)
                if (t, k) != (0, 0):
                    y_out[t, k] = away.astype(jnp.bfloat16)
                    sideways(t, k).start()
                else:

                    @pl.when(z == planes - 1)
                    def _():
                        y_out[t, k] = away.astype(jnp.bfloat16)
                        extra_down().start()
                        z_out[t, k] = held[t, k].astype(jnp.bfloat16)
                        down(t, k).start()

                    @pl.when(z == planes - 2)
                    def _():
                        extra_down().wait_recv()
                        y_out[t, k] = (away + extra_in[...].astype(jnp.float32)).astype(jnp.bfloat16)
                        sideways(t, k).start()

                    @pl.when(z < planes - 2)
                    def _():
                        y_out[t, k] = away.astype(jnp.bfloat16)
                        sideways(t, k).start()

    def dot(lhs, rhs):
        return lax.dot_general(lhs, rhs, NT, preferred_element_type=jnp.float32)

    def tiles(body):
        @pl.loop(0, half // TILE)
        def _(j):
            here = pl.ds(pl.multiple_of(j * TILE, TILE), TILE)
            there = (j * TILE // share, pl.ds(pl.multiple_of(j * TILE % share, TILE), TILE))
            body(here, there)

    for copy in locals_:
        copy.wait()

    def project_query(here, there):
        total[:, here] = dot(dq[...], mine[here, :feature])

    tiles(project_query)
    for copy in weights:
        copy.wait_recv()
    weight_swap.start()

    def project_query_far(here, there):
        total[:, here] += dot(dq_far[...], theirs[there[0], there[1], :feature])

    for t in range(planes):

        @pl.when(t <= z)
        def _(t=t):
            @pl.when(t == z)
            def _():
                query_swap.wait()
                weight_swap.wait()
                tiles(project_query_far)

            for k in kinds:

                @pl.when((z < planes - 1) | ((t, k) != (0, 0)))
                def _(k=k):
                    sideways(t, k).wait_recv()
                    held[t, k] += y_in[t, k].astype(jnp.float32)

                @pl.when(z < planes - 1)
                def _(k=k):
                    down(t, k).wait_recv()
                    held[t, k] += z_in[t, k].astype(jnp.float32)

                @pl.when((t < z) & ((z < planes - 1) | ((t, k) != (0, 0))))
                def _(k=k):
                    z_out[t, k] = held[t, k].astype(jnp.bfloat16)
                    down(t, k).start()

                @pl.when(t == z)
                def _(k=k):
                    dkv[k] = held[t, k].astype(jnp.bfloat16)
                    keyval_swap(k).start()

    def project_keyval(here, there):
        summed[:, here] = (
            total[:, here]
            + dot(dkv[0], mine[here, feature : feature + HD])
            + dot(dkv[1], mine[here, feature + HD :])
        ).astype(jnp.bfloat16)

    tiles(project_keyval)
    written = [
        pltpu.make_async_copy(summed, out_ref, write_sem.at[0]),
        pltpu.make_async_copy(theirs.at[:, :, feature:], far_ref, write_sem.at[1]),
    ]
    for copy in written:
        copy.start()
    for s in range(planes):

        @pl.when(z >= s)
        def _(s=s):
            for k in kinds:
                if s < planes - 1:

                    @pl.when(z < planes - 1)
                    def _(k=k):
                        up(s, k).wait_send()

                if (s, k) != (planes - 1, 1):
                    across(s, k).wait_send()
                between(s, k).wait_send()
                inward(s, k).wait_send()

                @pl.when((z < planes - 1) | ((s, k) != (0, 0)))
                def _(k=k):
                    sideways(s, k).wait_send()

                @pl.when(s < z)
                def _(k=k):
                    down(s, k).wait_send()

    @pl.when(z == planes - 2)
    def _():
        extra_up().wait_send()

    @pl.when(z == planes - 1)
    def _():
        extra_down().wait_send()

    for copy in weights:
        copy.wait_send()
    for k in kinds:
        keyval_swap(k).wait()
    for copy in written:
        copy.wait()


def finish_kernel(summed_ref, dkv_ref, far_ref, out_ref):
    out_ref[...] = (
        summed_ref[...].astype(jnp.float32)
        + lax.dot_general(dkv_ref[0], far_ref[:, :HD], NT, preferred_element_type=jnp.float32)
        + lax.dot_general(dkv_ref[1], far_ref[:, HD:], NT, preferred_element_type=jnp.float32)
    ).astype(jnp.bfloat16)


def finish(summed, dkv_far, far):
    rows, half = summed.shape
    wide = 2 * TILE
    column = pl.BlockSpec((rows, wide), lambda j: (0, j))
    return pl.pallas_call(
        finish_kernel,
        out_shape=jax.ShapeDtypeStruct(summed.shape, jnp.bfloat16),
        grid=(half // wide,),
        in_specs=[
            column,
            pl.BlockSpec(dkv_far.shape, lambda j: (0, 0, 0)),
            pl.BlockSpec((wide, far.shape[1]), lambda j: (j, 0)),
        ],
        out_specs=column,
        name="finish",
    )(summed, dkv_far, far)


def fused(selection, key, value, queries, output_grad, output_rows, lse, weights, planes):
    rows, width = queries.shape
    heads = width // HD
    half = weights[0].shape[0] // 2
    features = sum(weight.shape[1] for weight in weights)
    dma = pltpu.SemaphoreType.DMA
    vmem = pl.BlockSpec(memory_space=pltpu.VMEM)
    anywhere = pl.BlockSpec(memory_space=pl.ANY)

    def half_type(*shape):
        return pltpu.VMEM(shape, jnp.bfloat16)

    def full_type(*shape):
        return pltpu.VMEM(shape, jnp.float32)

    slots = half_type(planes, 2, rows, HD)
    summed, dkv_far, far = pl.pallas_call(
        functools.partial(fused_kernel, planes),
        out_shape=(
            jax.ShapeDtypeStruct((rows, half), jnp.bfloat16),
            jax.ShapeDtypeStruct((2, rows, HD), jnp.bfloat16),
            jax.ShapeDtypeStruct((2, half // 2, 2 * HD), jnp.bfloat16),
        ),
        in_specs=[pl.BlockSpec(memory_space=pltpu.SMEM)] + [vmem] * 6 + [anywhere] * 3,
        out_specs=(anywhere,) * 3,
        scratch_shapes=[
            half_type(planes, 2, 2, 2, rows, HD),
            half_type(planes, 2, 2, 2, rows, HD),
            full_type(heads, rows),
            full_type(2 * heads, HD, rows),
            half_type(4, 2, rows, HD),
            half_type(rows, width),
            half_type(rows, width),
            half_type(half, features),
            half_type(2, half // 2, features),
            full_type(rows, half),
            half_type(planes, 2, 2, rows, HD),
            slots, slots, slots, slots,
            full_type(planes, 2, rows, HD),
            half_type(2, rows, HD),
            half_type(rows, half),
            half_type(rows, HD),
        ] + [dma((planes, 2))] * 12 + [dma((3,)), dma((3,)), dma((3,)), dma(()), dma(()), dma((3,)), dma((3,)), dma((2,)), dma((2,)), dma((2,))],
        compiler_params=pltpu.CompilerParams(
            collective_id=2, has_side_effects=True, vmem_limit_bytes=VMEM_LIMIT
        ),
        name="fused",
    )(selection, key, value, queries, output_grad, output_rows, lse, *weights)
    return finish(summed, dkv_far, far.reshape(half, 2 * HD))


def on_device(
    queries, key_rows, value_rows, output_rows, output_grad, log_normalizer,
    selection, query_weight, key_weight, value_weight,
):
    position = lax.axis_index("ctx")
    contexts = lax.axis_size("ctx")
    groups = lax.axis_size("grp")
    planes = contexts // 4
    if groups == 2:
        weights = (query_weight, key_weight, value_weight)
        lse = log_normalizer.T
        return fused(
            selection.T, key_rows, value_rows, queries, output_grad, output_rows, lse, weights, planes
        )

    blocks = gather_blocks(jnp.concatenate([key_rows, value_rows], axis=1), planes)
    row = lax.dynamic_index_in_dim(selection, position, 0, keepdims=False).astype(jnp.int32)
    chosen = jnp.concatenate([position[None].astype(jnp.int32), row])
    usable = jnp.concatenate([jnp.ones((1,), jnp.int32), (row < position).astype(jnp.int32)])
    grad_query, part = attend(
        chosen, usable, queries, output_grad, output_rows, log_normalizer.T, blocks
    )
    grad_keyval = scatter_blocks(part, planes)
    dot = functools.partial(lax.dot_general, dimension_numbers=NT, preferred_element_type=jnp.float32)
    combined = dot(grad_query, query_weight)
    combined = combined + dot(grad_keyval[:, :HD], key_weight)
    combined = combined + dot(grad_keyval[:, HD:], value_weight)
    return lax.psum_scatter(combined.astype(jnp.bfloat16), "grp", scatter_dimension=1, tiled=True)


def solution(mesh):
    return jax.shard_map(
        on_device,
        mesh=mesh,
        in_specs=(
            P("ctx", "grp"),
            P("ctx", "grp"),
            P("ctx", "grp"),
            P("ctx", "grp"),
            P("ctx", "grp"),
            P("ctx", "grp"),
            P(),
            P(None, "grp"),
            P(None, "grp"),
            P(None, "grp"),
        ),
        out_specs=P("ctx", "grp"),
        check_vma=False,
    )
```

```python
import functools
import math

import jax
import jax.numpy as jnp
from jax import lax
from jax.experimental import pallas as pl
from jax.experimental.pallas import tpu as pltpu
from jax.sharding import PartitionSpec as P

HD = 128
BLOCK = 512
TOPK = 3
MESH = pl.DeviceIdType.MESH
SCALE = float(HD) ** (-0.5)
LOG2E = math.log2(math.e)
VMEM_LIMIT = 56 * 1024 * 1024
NT = (((1,), (1,)), ((), ()))
NN = (((1,), (0,)), ((), ()))


def place():
    me = lax.axis_index("ctx")
    return me, me // 4, (me // 2) % 2, me % 2


def sibling_of(me, core):
    return me + 1 - 2 * core


def beside(me, column):
    return me + 2 - 4 * column


def remote(src, dst, send, recv, target):
    return pltpu.make_async_remote_copy(
        src_ref=src, dst_ref=dst, send_sem=send, recv_sem=recv,
        device_id={"ctx": target}, device_id_type=MESH,
    )


def greet(target):
    pl.semaphore_signal(
        pltpu.get_barrier_semaphore(), inc=1, device_id={"ctx": target}, device_id_type=MESH
    )


def gather_kernel(planes, kv_ref, all_ref, own_sem, z_send, z_recv, y_send, y_recv, c_send, c_recv):
    me, z, y, c = place()
    sibling, side = sibling_of(me, c), beside(me, y)
    greet(sibling)
    greet(side)

    @pl.when(z > 0)
    def _():
        greet(me - 4)

    own = pltpu.make_async_copy(kv_ref, all_ref.at[z, c, y], own_sem)
    own.start()
    pl.semaphore_wait(pltpu.get_barrier_semaphore(), 2 + (z < planes - 1).astype(jnp.int32))

    def up(s):
        src = kv_ref if s == 0 else all_ref.at[z - s, c, y]
        return remote(src, all_ref.at[z - s, c, y], z_send.at[s], z_recv.at[s + 1], me + 4)

    def from_below(s):
        slot = all_ref.at[z - s, c, y]
        return remote(slot, slot, z_send.at[s], z_recv.at[s], me)

    def across(s):
        src = kv_ref if s == 0 else all_ref.at[z - s, c, y]
        return remote(src, all_ref.at[z - s, c, y], y_send.at[s], y_recv.at[s], side)

    def between(s):
        pair = all_ref.at[z - s, c]
        return remote(pair, pair, c_send.at[s], c_recv.at[s], sibling)

    for s in range(planes + 1):
        if s < planes:

            @pl.when(z >= s)
            def _(s=s):
                if s > 0:
                    from_below(s).wait_recv()
                if s < planes - 1:

                    @pl.when(z < planes - 1)
                    def _():
                        up(s).start()

                across(s).start()

        if s == 0:
            own.wait()
        else:

            @pl.when(z >= s - 1)
            def _(s=s):
                across(s - 1).wait_recv()
                between(s - 1).start()

    for s in range(planes):

        @pl.when(z >= s)
        def _(s=s):
            if s < planes - 1:

                @pl.when(z < planes - 1)
                def _():
                    up(s).wait_send()

            across(s).wait_send()
            between(s).wait()


def gather_blocks(kv, planes):
    shape = (planes, 2, 2) + kv.shape
    dma = pltpu.SemaphoreType.DMA
    return pl.pallas_call(
        functools.partial(gather_kernel, planes),
        out_shape=jax.ShapeDtypeStruct(shape, kv.dtype),
        in_specs=[pl.BlockSpec(memory_space=pl.ANY)],
        out_specs=pl.BlockSpec(memory_space=pl.ANY),
        scratch_shapes=[dma(())] + [dma((planes,))] * 6,
        compiler_params=pltpu.CompilerParams(collective_id=0, has_side_effects=True),
        name="gather_blocks",
    )(kv)


def attend_kernel(
    chosen_ref, usable_ref, q_ref, do_ref, o_ref, lse_ref, kv_ref,
    dq_ref, part_ref, delta, dq_sum,
):
    slot = pl.program_id(0)
    heads = q_ref.shape[1] // HD

    def columns(h):
        return slice(h * HD, (h + 1) * HD)

    @pl.when(slot == 0)
    def _():
        part_ref[...] = jnp.zeros_like(part_ref)
        dq_sum[...] = jnp.zeros_like(dq_sum)
        for h in range(heads):
            product = do_ref[:, columns(h)].astype(jnp.float32) * o_ref[:, columns(h)].astype(jnp.float32)
            delta[h : h + 1, :] = jnp.sum(product.T, axis=0, keepdims=True)

    def pair(diagonal):
        key = kv_ref[0, 0, 0, :, :HD]
        value = kv_ref[0, 0, 0, :, HD:]
        key_t = key.astype(jnp.float32).T.astype(jnp.bfloat16)
        if diagonal:
            key_pos = lax.broadcasted_iota(jnp.int32, (BLOCK, BLOCK), 0)
            query_pos = lax.broadcasted_iota(jnp.int32, (BLOCK, BLOCK), 1)
            seen = key_pos <= query_pos
        dk = jnp.zeros((BLOCK, HD), jnp.float32)
        dv = jnp.zeros((BLOCK, HD), jnp.float32)
        for h in range(heads):
            query, cotangent = q_ref[:, columns(h)], do_ref[:, columns(h)]
            scores = lax.dot_general(key, query, NT, preferred_element_type=jnp.float32)
            probs = jnp.exp2(scores * (SCALE * LOG2E) - lse_ref[h : h + 1, :] * LOG2E)
            if diagonal:
                probs = jnp.where(seen, probs, 0.0)
            prob_grad = lax.dot_general(value, cotangent, NT, preferred_element_type=jnp.float32)
            score_half = (probs * (prob_grad - delta[h : h + 1, :])).astype(jnp.bfloat16)
            probs_half = probs.astype(jnp.bfloat16)
            dv = dv + lax.dot_general(probs_half, cotangent, NN, preferred_element_type=jnp.float32)
            dk = dk + lax.dot_general(score_half, query, NN, preferred_element_type=jnp.float32)
            dq_sum[h] += lax.dot_general(key_t, score_half, NN, preferred_element_type=jnp.float32)
        block = chosen_ref[slot]
        at = (block // 4, block % 2, (block // 2) % 2)
        part_ref[at + (slice(None), slice(0, HD))] = (dk * SCALE).astype(jnp.bfloat16)
        part_ref[at + (slice(None), slice(HD, 2 * HD))] = dv.astype(jnp.bfloat16)

    @pl.when(slot == 0)
    def _():
        pair(True)

    @pl.when((slot > 0) & (usable_ref[slot] > 0))
    def _():
        pair(False)

    @pl.when(slot == TOPK)
    def _():
        for h in range(heads):
            dq_ref[:, columns(h)] = (dq_sum[h] * SCALE).T.astype(jnp.bfloat16)


def attend(chosen, usable, queries, output_grad, output_rows, lse, blocks):
    rows, width = queries.shape
    heads = width // HD
    whole = lambda s, chosen, usable: (0, 0)
    wide = pl.BlockSpec((rows, width), whole)
    return pl.pallas_call(
        attend_kernel,
        out_shape=(
            jax.ShapeDtypeStruct((rows, width), jnp.bfloat16),
            jax.ShapeDtypeStruct(blocks.shape, jnp.bfloat16),
        ),
        grid_spec=pltpu.PrefetchScalarGridSpec(
            num_scalar_prefetch=2,
            grid=(TOPK + 1,),
            in_specs=[
                wide, wide, wide,
                pl.BlockSpec((heads, rows), whole),
                pl.BlockSpec(
                    (1, 1, 1) + blocks.shape[3:],
                    lambda s, chosen, usable: (
                        chosen[s] // 4, chosen[s] % 2, (chosen[s] // 2) % 2, 0, 0,
                    ),
                ),
            ],
            out_specs=[wide, pl.BlockSpec(blocks.shape, lambda s, chosen, usable: (0,) * 5)],
            scratch_shapes=[
                pltpu.VMEM((heads, rows), jnp.float32),
                pltpu.VMEM((heads, HD, rows), jnp.float32),
            ],
        ),
        compiler_params=pltpu.CompilerParams(vmem_limit_bytes=VMEM_LIMIT),
        cost_estimate=pl.CostEstimate(flops=6 * 10**9, bytes_accessed=10 * 2**20, transcendentals=4 * 2**20),
        name="attend",
    )(chosen, usable, queries, output_grad, output_rows, lse, blocks)


def scatter_kernel(
    planes, part_ref, out_ref, c_in, y_in, z_in, y_out, z_out, held,
    z_send, z_recv, y_send, y_recv, c_send, c_recv,
):
    me, z, y, c = place()
    sibling, side = sibling_of(me, c), beside(me, y)
    greet(sibling)
    greet(side)

    @pl.when(z < planes - 1)
    def _():
        greet(me + 4)

    pl.semaphore_wait(pltpu.get_barrier_semaphore(), 2 + (z > 0).astype(jnp.int32))

    def between(t):
        return remote(part_ref.at[t, 1 - c], c_in.at[t], c_send.at[t], c_recv.at[t], sibling)

    def across(t):
        return remote(y_out.at[t], y_in.at[t], y_send.at[t], y_recv.at[t], side)

    def down(t):
        return remote(z_out.at[t], z_in.at[t], z_send.at[t], z_recv.at[t], me - 4)

    for t in range(planes):

        @pl.when(t <= z)
        def _(t=t):
            between(t).start()

    for t in range(planes):

        @pl.when(t <= z)
        def _(t=t):
            between(t).wait_recv()
            y_out[t] = (
                part_ref[t, c, 1 - y].astype(jnp.float32) + c_in[t, 1 - y].astype(jnp.float32)
            ).astype(jnp.bfloat16)
            across(t).start()
            held[t] = part_ref[t, c, y].astype(jnp.float32) + c_in[t, y].astype(jnp.float32)

    for t in range(planes):

        @pl.when(t <= z)
        def _(t=t):
            across(t).wait_recv()
            held[t] += y_in[t].astype(jnp.float32)

            @pl.when(z < planes - 1)
            def _():
                down(t).wait_recv()
                held[t] += z_in[t].astype(jnp.float32)

            @pl.when(t < z)
            def _():
                z_out[t] = held[t].astype(jnp.bfloat16)
                down(t).start()

            @pl.when(t == z)
            def _():
                out_ref[...] = held[t].astype(jnp.bfloat16)

    for t in range(planes):

        @pl.when(t <= z)
        def _(t=t):
            between(t).wait_send()
            across(t).wait_send()

            @pl.when(t < z)
            def _():
                down(t).wait_send()


def scatter_blocks(part, planes):
    block = part.shape[3:]
    dma = pltpu.SemaphoreType.DMA
    slots = pltpu.VMEM((planes,) + block, jnp.bfloat16)
    return pl.pallas_call(
        functools.partial(scatter_kernel, planes),
        out_shape=jax.ShapeDtypeStruct(block, jnp.bfloat16),
        in_specs=[pl.BlockSpec(memory_space=pltpu.VMEM)],
        out_specs=pl.BlockSpec(memory_space=pltpu.VMEM),
        scratch_shapes=[
            pltpu.VMEM((planes, 2) + block, jnp.bfloat16),
            slots, slots, slots, slots,
            pltpu.VMEM((planes,) + block, jnp.float32),
        ] + [dma((planes,))] * 6,
        compiler_params=pltpu.CompilerParams(
            collective_id=1, has_side_effects=True, vmem_limit_bytes=VMEM_LIMIT
        ),
        cost_estimate=pl.CostEstimate(flops=10**9, bytes_accessed=100 * 2**20, transcendentals=0),
        name="scatter_blocks",
    )(part)


def toward(src, dst, send, recv):
    return pltpu.make_async_remote_copy(
        src_ref=src, dst_ref=dst, send_sem=send, recv_sem=recv,
        device_id={"grp": 1 - lax.axis_index("grp")}, device_id_type=MESH,
    )


def greet_group():
    pl.semaphore_signal(
        pltpu.get_barrier_semaphore(), inc=1,
        device_id={"grp": 1 - lax.axis_index("grp")}, device_id_type=MESH,
    )


def columns(h):
    return slice(h * HD, (h + 1) * HD)


def part_gradients(key, value, q_ref, do_ref, lse_ref, delta_ref, dq_sum, diagonal=None, usable=None):
    heads = q_ref.shape[1] // HD
    count, rows = key.shape[0], q_ref.shape[0]
    key_t = key.astype(jnp.float32).T.astype(jnp.bfloat16)
    if diagonal is not None:
        key_pos = lax.broadcasted_iota(jnp.int32, (count, rows), 0) + diagonal
        query_pos = lax.broadcasted_iota(jnp.int32, (count, rows), 1)
        seen = key_pos <= query_pos
    dk = jnp.zeros((count, HD), jnp.float32)
    dv = jnp.zeros((count, HD), jnp.float32)
    for h in range(heads):
        query, cotangent = q_ref[:, columns(h)], do_ref[:, columns(h)]
        scores = lax.dot_general(key, query, NT, preferred_element_type=jnp.float32)
        probs = jnp.exp2(scores * (SCALE * LOG2E) - lse_ref[h : h + 1, :] * LOG2E)
        if diagonal is not None:
            probs = jnp.where(seen, probs, 0.0)
        prob_grad = lax.dot_general(value, cotangent, NT, preferred_element_type=jnp.float32)
        score_half = (probs * (prob_grad - delta_ref[h : h + 1, :])).astype(jnp.bfloat16)
        probs_half = probs.astype(jnp.bfloat16)
        dv = dv + lax.dot_general(probs_half, cotangent, NN, preferred_element_type=jnp.float32)
        dk = dk + lax.dot_general(score_half, query, NN, preferred_element_type=jnp.float32)
        dq = lax.dot_general(key_t, score_half, NN, preferred_element_type=jnp.float32)
        if usable is not None:
            dq = jnp.where(usable, dq, 0.0)
        dq_sum[h] = dq if diagonal == 0 else dq_sum[h] + dq
    return (dk * SCALE).astype(jnp.bfloat16), dv.astype(jnp.bfloat16)


TILE = 256


def fused_kernel(
    planes, selection_ref, key_ref, value_ref, q_ref, do_ref, o_ref, lse_ref, wq_ref, wk_ref, wv_ref,
    out_ref, dkv_far, far_ref,
    blocks, part, delta, dq_sum, picked, dq, dq_far, mine, theirs, total,
    c_in, y_in, z_in, y_out, z_out, held, dkv, summed, extra_in,
    gz_send, gz_recv, gy_send, gy_recv, gc_send, gc_recv,
    sz_send, sz_recv, sy_send, sy_recv, sc_send, sc_recv,
    local_sem, w_send, w_recv, swap_send, swap_recv, x_send, x_recv,
    extra_send, extra_recv, write_sem,
):
    me, z, y, c = place()
    group = lax.axis_index("grp")
    sibling, side = sibling_of(me, c), beside(me, y)
    heads = q_ref.shape[1] // HD
    feature = q_ref.shape[1]
    half = out_ref.shape[1]
    share = half // 2
    piece = q_ref.shape[0] // 2
    pieces = range(4)
    early = (0, 1)
    late = (2, 3)

    greet(sibling)
    greet(side)
    greet_group()

    @pl.when(z > 0)
    def _():
        greet(me - 4)

    @pl.when(z < planes - 1)
    def _():
        greet(me + 4)

    local_rows = pl.ds(pl.multiple_of(group * half, half), half)
    away_rows = pl.ds(pl.multiple_of((1 - group) * half + c * share, share), share)
    locals_, weights = [], []
    first = 0
    for i, weight in enumerate((wq_ref, wk_ref, wv_ref)):
        last = first + weight.shape[1]
        locals_.append(
            pltpu.make_async_copy(weight.at[local_rows], mine.at[:, first:last], local_sem.at[i])
        )
        weights.append(
            toward(weight.at[away_rows], theirs.at[c, :, first:last], w_send.at[i], w_recv.at[i])
        )
        first = last
    weight_swap = remote(theirs.at[c], theirs.at[c], swap_send, swap_recv, sibling)

    for r in range(2):
        blocks[z, c, 2 * r, y] = key_ref[r * piece : (r + 1) * piece, :]
        blocks[z, c, 2 * r + 1, y] = value_ref[r * piece : (r + 1) * piece, :]
    pl.semaphore_wait(
        pltpu.get_barrier_semaphore(),
        3 + (z > 0).astype(jnp.int32) + (z < planes - 1).astype(jnp.int32),
    )

    def up(s, k):
        slot = blocks.at[z - s, c, k, y]
        return remote(slot, slot, gz_send.at[s, k], gz_recv.at[s + 1, k], me + 4)

    def from_below(s, k):
        slot = blocks.at[z - s, c, k, y]
        return remote(slot, slot, gz_send.at[s, k], gz_recv.at[s, k], me)

    def across(s, k):
        slot = blocks.at[z - s, c, k, y]
        return remote(slot, slot, gy_send.at[s, k], gy_recv.at[s, k], side)

    def between(s, k):
        pair = blocks.at[z - s, c, k]
        return remote(pair, pair, gc_send.at[s, k], gc_recv.at[s, k], sibling)

    def extra_up(k):
        slot = blocks.at[0, c, k, 1 - y]
        return remote(slot, slot, extra_send.at[k], extra_recv.at[k], me + 4)

    def gradients(key, value, **kind):
        return part_gradients(key, value, q_ref, do_ref, lse_ref, delta, dq_sum, **kind)

    def stored(block, r):
        at = (block // 4, block % 2)
        column = ((block // 2) % 2,)
        return blocks[at + (2 * r,) + column], blocks[at + (2 * r + 1,) + column]

    for s in range(planes + 1):
        for k in pieces:
            if s < planes:

                @pl.when(z >= s)
                def _(s=s, k=k):
                    if s > 0:
                        from_below(s, k).wait_recv()
                    if s < planes - 1:

                        @pl.when(z < planes - 1)
                        def _():
                            up(s, k).start()

                    if s < planes - 1 or k in early:
                        across(s, k).start()

            if s > 0:

                @pl.when(z >= s - 1)
                def _(s=s, k=k):
                    if s < planes or k in early:
                        across(s - 1, k).wait_recv()
                    else:
                        extra_up(k).wait_recv()
                    if s == planes - 1 and k in late:

                        @pl.when(z == planes - 2)
                        def _():
                            extra_up(k).start()

                    between(s - 1, k).start()

        if s == 0:
            for copy in weights + locals_:
                copy.start()
            for h in range(heads):
                product = do_ref[:, columns(h)].astype(jnp.float32) * o_ref[:, columns(h)].astype(jnp.float32)
                delta[h : h + 1, :] = jnp.sum(product.T, axis=0, keepdims=True)
            for r in range(2):
                rows = slice(r * piece, (r + 1) * piece)
                dk, dv = gradients(key_ref[rows, :], value_ref[rows, :], diagonal=r * piece)
                picked[0, 2 * r] = dk
                picked[0, 2 * r + 1] = dv

        if s == 2:
            for k in pieces:
                between(0, k).wait_recv()

                @pl.when(z >= 1)
                def _(k=k):
                    between(1, k).wait_recv()

            @pl.when(me > 0)
            def _():
                for r in range(2):
                    dk, dv = gradients(*stored(me - 1, r))
                    picked[1, 2 * r] = dk
                    picked[1, 2 * r + 1] = dv

    for s in range(2, planes):

        @pl.when(z >= s)
        def _(s=s):
            for k in pieces:
                between(s, k).wait_recv()

    picks = [selection_ref[column, me] for column in range(TOPK)]
    others = [
        jnp.where(picks[0] == me - 1, picks[1], picks[0]),
        jnp.where(picks[2] == me - 1, picks[1], picks[2]),
    ]

    def chosen_gradients(i, r):
        usable = others[i] < me
        key, value = stored(jnp.where(usable, others[i], me), r)
        dk, dv = gradients(key, value, usable=usable)
        picked[2 + i, 2 * r] = dk
        picked[2 + i, 2 * r + 1] = dv

    def inward(t, r):
        pair = pl.ds(2 * r, 2)
        return remote(
            part.at[t, 1 - c, pair], c_in.at[t, pair], sc_send.at[t, r], sc_recv.at[t, r], sibling
        )

    def sideways(t, k):
        return remote(y_out.at[t, k], y_in.at[t, k], sy_send.at[t, k], sy_recv.at[t, k], side)

    def down(t, k):
        return remote(z_out.at[t, k], z_in.at[t, k], sz_send.at[t, k], sz_recv.at[t, k], me - 4)

    def extra_down(k):
        return remote(y_out.at[0, k], extra_in.at[k], extra_send.at[k], extra_recv.at[2 + k], me - 4)

    def spot(k):
        return slice(k // 2 * piece, (k // 2 + 1) * piece), slice(k % 2 * HD, (k % 2 + 1) * HD)

    def keyval_swap(k):
        return toward(dkv.at[spot(k)], dkv_far.at[spot(k)], x_send.at[k], x_recv.at[k])

    def place_partials(t, core, r):
        for column in range(2):
            block = t * 4 + column * 2 + core
            for k in (2 * r, 2 * r + 1):
                nothing = jnp.zeros((piece, HD), jnp.bfloat16)
                chosen = jnp.where((others[0] == block) & (block < me), picked[2, k], nothing)
                chosen = jnp.where((others[1] == block) & (block < me), picked[3, k], chosen)
                part[t, core, k, column] = chosen

                @pl.when(block == me)
                def _(k=k, column=column):
                    part[t, core, k, column] = picked[0, k]

                @pl.when(block == me - 1)
                def _(k=k, column=column):
                    part[t, core, k, column] = picked[1, k]

    def send_inward(r):
        for t in range(planes):

            @pl.when(t <= z)
            def _(t=t):
                place_partials(t, 1 - c, r)
                inward(t, r).start()

        for t in range(planes):

            @pl.when(t <= z)
            def _(t=t):
                place_partials(t, c, r)

    def send_sideways(t, r):
        @pl.when(t <= z)
        def _():
            inward(t, r).wait_recv()
            for k in (2 * r, 2 * r + 1):
                away = part[t, c, k, 1 - y].astype(jnp.float32) + c_in[t, k, 1 - y].astype(jnp.float32)
                held[t, k] = part[t, c, k, y].astype(jnp.float32) + c_in[t, k, y].astype(jnp.float32)
                if t > 0 or k in late:
                    y_out[t, k] = away.astype(jnp.bfloat16)
                    sideways(t, k).start()
                else:

                    @pl.when(z == planes - 1)
                    def _(k=k, away=away):
                        y_out[t, k] = away.astype(jnp.bfloat16)
                        extra_down(k).start()
                        z_out[t, k] = held[t, k].astype(jnp.bfloat16)
                        down(t, k).start()

                    @pl.when(z == planes - 2)
                    def _(k=k, away=away):
                        extra_down(k).wait_recv()
                        y_out[t, k] = (away + extra_in[k].astype(jnp.float32)).astype(jnp.bfloat16)
                        sideways(t, k).start()

                    @pl.when(z < planes - 2)
                    def _(k=k, away=away):
                        y_out[t, k] = away.astype(jnp.bfloat16)
                        sideways(t, k).start()

    first = [(t, 0) for t in range(1, planes - 1)] + [(0, 0)]
    second = [(0, 1), (planes - 1, 0)] + [(t, 1) for t in range(1, planes)]
    chosen_gradients(0, 0)
    chosen_gradients(1, 0)
    send_inward(0)
    chosen_gradients(0, 1)
    for t, r in first:
        send_sideways(t, r)
    chosen_gradients(1, 1)
    send_inward(1)
    for h in range(heads):
        dq[:, columns(h)] = (dq_sum[h] * SCALE).T.astype(jnp.bfloat16)
    query_swap = toward(dq, dq_far, x_send.at[4], x_recv.at[4])
    query_swap.start()
    for t, r in second:
        send_sideways(t, r)

    def dot(lhs, rhs):
        return lax.dot_general(lhs, rhs, NT, preferred_element_type=jnp.float32)

    def tiles(body):
        @pl.loop(0, half // TILE)
        def _(j):
            here = pl.ds(pl.multiple_of(j * TILE, TILE), TILE)
            there = (j * TILE // share, pl.ds(pl.multiple_of(j * TILE % share, TILE), TILE))
            body(here, there)

    for copy in locals_:
        copy.wait()

    def project_query(here, there):
        total[:, here] = dot(dq[...], mine[here, :feature])

    tiles(project_query)
    def project_query_far(here, there):
        total[:, here] += dot(dq_far[...], theirs[there[0], there[1], :feature])

    for t, r in [(t, 0) for t in range(planes - 1)] + second:
        if (t, r) == second[0]:
            for copy in weights:
                copy.wait_recv()
            weight_swap.start()

        @pl.when(t <= z)
        def _(t=t, r=r):
            if r == 1:

                @pl.when(t == z)
                def _():
                    query_swap.wait()
                    weight_swap.wait()
                    tiles(project_query_far)

            for k in (2 * r, 2 * r + 1):
                direct = t == 0 and k in early

                @pl.when((z < planes - 1) | (not direct))
                def _(k=k):
                    sideways(t, k).wait_recv()
                    held[t, k] += y_in[t, k].astype(jnp.float32)

                @pl.when(z < planes - 1)
                def _(k=k):
                    down(t, k).wait_recv()
                    held[t, k] += z_in[t, k].astype(jnp.float32)

                @pl.when((t < z) & ((z < planes - 1) | (not direct)))
                def _(k=k):
                    z_out[t, k] = held[t, k].astype(jnp.bfloat16)
                    down(t, k).start()

                @pl.when(t == z)
                def _(k=k):
                    dkv[spot(k)] = held[t, k].astype(jnp.bfloat16)
                    keyval_swap(k).start()

    def project_keyval(here, there):
        summed[:, here] = (
            total[:, here]
            + dot(dkv[...], mine[here, feature:])
        ).astype(jnp.bfloat16)

    tiles(project_keyval)
    written = [
        pltpu.make_async_copy(summed, out_ref, write_sem.at[0]),
        pltpu.make_async_copy(theirs.at[:, :, feature:], far_ref, write_sem.at[1]),
    ]
    for copy in written:
        copy.start()
    for s in range(planes):

        @pl.when(z >= s)
        def _(s=s):
            for r in range(2):
                inward(s, r).wait_send()
            for k in pieces:
                if s < planes - 1:

                    @pl.when(z < planes - 1)
                    def _(k=k):
                        up(s, k).wait_send()

                if s < planes - 1 or k in early:
                    across(s, k).wait_send()
                between(s, k).wait_send()

                @pl.when((z < planes - 1) | (not (s == 0 and k in early)))
                def _(k=k):
                    sideways(s, k).wait_send()

                @pl.when(s < z)
                def _(k=k):
                    down(s, k).wait_send()

    @pl.when(z == planes - 2)
    def _():
        for k in late:
            extra_up(k).wait_send()

    @pl.when(z == planes - 1)
    def _():
        for k in early:
            extra_down(k).wait_send()

    for copy in weights:
        copy.wait_send()
    for k in pieces:
        keyval_swap(k).wait()
    for copy in written:
        copy.wait()


def finish_kernel(summed_ref, dkv_ref, far_ref, out_ref):
    out_ref[...] = (
        summed_ref[...].astype(jnp.float32)
        + lax.dot_general(dkv_ref[...], far_ref[...], NT, preferred_element_type=jnp.float32)
    ).astype(jnp.bfloat16)


def finish(summed, dkv_far, far):
    rows, half = summed.shape
    wide = 2 * TILE
    column = pl.BlockSpec((rows, wide), lambda j: (0, j))
    return pl.pallas_call(
        finish_kernel,
        out_shape=jax.ShapeDtypeStruct(summed.shape, jnp.bfloat16),
        grid=(half // wide,),
        in_specs=[
            column,
            pl.BlockSpec(dkv_far.shape, lambda j: (0, 0)),
            pl.BlockSpec((wide, far.shape[1]), lambda j: (j, 0)),
        ],
        out_specs=column,
        name="finish",
    )(summed, dkv_far, far)


def fused(selection, key, value, queries, output_grad, output_rows, lse, weights, planes):
    rows, width = queries.shape
    heads = width // HD
    half = weights[0].shape[0] // 2
    features = sum(weight.shape[1] for weight in weights)
    dma = pltpu.SemaphoreType.DMA
    vmem = pl.BlockSpec(memory_space=pltpu.VMEM)
    anywhere = pl.BlockSpec(memory_space=pl.ANY)

    def half_type(*shape):
        return pltpu.VMEM(shape, jnp.bfloat16)

    def full_type(*shape):
        return pltpu.VMEM(shape, jnp.float32)

    piece = rows // 2
    slots = half_type(planes, 4, piece, HD)
    summed, dkv_far, far = pl.pallas_call(
        functools.partial(fused_kernel, planes),
        out_shape=(
            jax.ShapeDtypeStruct((rows, half), jnp.bfloat16),
            jax.ShapeDtypeStruct((rows, 2 * HD), jnp.bfloat16),
            jax.ShapeDtypeStruct((2, half // 2, 2 * HD), jnp.bfloat16),
        ),
        in_specs=[pl.BlockSpec(memory_space=pltpu.SMEM)] + [vmem] * 6 + [anywhere] * 3,
        out_specs=(anywhere,) * 3,
        scratch_shapes=[
            half_type(planes, 2, 4, 2, piece, HD),
            half_type(planes, 2, 4, 2, piece, HD),
            full_type(heads, rows),
            full_type(heads, HD, rows),
            half_type(4, 4, piece, HD),
            half_type(rows, width),
            half_type(rows, width),
            half_type(half, features),
            half_type(2, half // 2, features),
            full_type(rows, half),
            half_type(planes, 4, 2, piece, HD),
            slots, slots, slots, slots,
            full_type(planes, 4, piece, HD),
            half_type(rows, 2 * HD),
            half_type(rows, half),
            half_type(2, piece, HD),
        ] + [dma((planes, 4))] * 12 + [
            dma((3,)), dma((3,)), dma((3,)), dma(()), dma(()), dma((5,)), dma((5,)), dma((4,)), dma((4,)), dma((2,)),
        ],
        compiler_params=pltpu.CompilerParams(
            collective_id=2, has_side_effects=True, vmem_limit_bytes=VMEM_LIMIT
        ),
        name="fused",
    )(selection, key, value, queries, output_grad, output_rows, lse, *weights)
    return finish(summed, dkv_far, far.reshape(half, 2 * HD))


def on_device(
    queries, key_rows, value_rows, output_rows, output_grad, log_normalizer,
    selection, query_weight, key_weight, value_weight,
):
    position = lax.axis_index("ctx")
    contexts = lax.axis_size("ctx")
    groups = lax.axis_size("grp")
    planes = contexts // 4
    if groups == 2:
        weights = (query_weight, key_weight, value_weight)
        lse = log_normalizer.T
        return fused(
            selection.T, key_rows, value_rows, queries, output_grad, output_rows, lse, weights, planes
        )

    blocks = gather_blocks(jnp.concatenate([key_rows, value_rows], axis=1), planes)
    row = lax.dynamic_index_in_dim(selection, position, 0, keepdims=False).astype(jnp.int32)
    chosen = jnp.concatenate([position[None].astype(jnp.int32), row])
    usable = jnp.concatenate([jnp.ones((1,), jnp.int32), (row < position).astype(jnp.int32)])
    grad_query, part = attend(
        chosen, usable, queries, output_grad, output_rows, log_normalizer.T, blocks
    )
    grad_keyval = scatter_blocks(part, planes)
    dot = functools.partial(lax.dot_general, dimension_numbers=NT, preferred_element_type=jnp.float32)
    combined = dot(grad_query, query_weight)
    combined = combined + dot(grad_keyval[:, :HD], key_weight)
    combined = combined + dot(grad_keyval[:, HD:], value_weight)
    return lax.psum_scatter(combined.astype(jnp.bfloat16), "grp", scatter_dimension=1, tiled=True)


def solution(mesh):
    return jax.shard_map(
        on_device,
        mesh=mesh,
        in_specs=(
            P("ctx", "grp"),
            P("ctx", "grp"),
            P("ctx", "grp"),
            P("ctx", "grp"),
            P("ctx", "grp"),
            P("ctx", "grp"),
            P(),
            P(None, "grp"),
            P(None, "grp"),
            P(None, "grp"),
        ),
        out_specs=P("ctx", "grp"),
        check_vma=False,
    )
```

```python
import functools
import math

import jax
import jax.numpy as jnp
from jax import lax
from jax.experimental import pallas as pl
from jax.experimental.pallas import tpu as pltpu
from jax.sharding import PartitionSpec as P

HD = 128
BLOCK = 512
TOPK = 3
MESH = pl.DeviceIdType.MESH
SCALE = float(HD) ** (-0.5)
LOG2E = math.log2(math.e)
VMEM_LIMIT = 56 * 1024 * 1024
NT = (((1,), (1,)), ((), ()))
NN = (((1,), (0,)), ((), ()))


def place():
    me = lax.axis_index("ctx")
    return me, me // 4, (me // 2) % 2, me % 2


def sibling_of(me, core):
    return me + 1 - 2 * core


def beside(me, column):
    return me + 2 - 4 * column


def remote(src, dst, send, recv, target):
    return pltpu.make_async_remote_copy(
        src_ref=src, dst_ref=dst, send_sem=send, recv_sem=recv,
        device_id={"ctx": target}, device_id_type=MESH,
    )


def greet(target):
    pl.semaphore_signal(
        pltpu.get_barrier_semaphore(), inc=1, device_id={"ctx": target}, device_id_type=MESH
    )


def gather_kernel(planes, kv_ref, all_ref, own_sem, z_send, z_recv, y_send, y_recv, c_send, c_recv):
    me, z, y, c = place()
    sibling, side = sibling_of(me, c), beside(me, y)
    greet(sibling)
    greet(side)

    @pl.when(z > 0)
    def _():
        greet(me - 4)

    own = pltpu.make_async_copy(kv_ref, all_ref.at[z, c, y], own_sem)
    own.start()
    pl.semaphore_wait(pltpu.get_barrier_semaphore(), 2 + (z < planes - 1).astype(jnp.int32))

    def up(s):
        src = kv_ref if s == 0 else all_ref.at[z - s, c, y]
        return remote(src, all_ref.at[z - s, c, y], z_send.at[s], z_recv.at[s + 1], me + 4)

    def from_below(s):
        slot = all_ref.at[z - s, c, y]
        return remote(slot, slot, z_send.at[s], z_recv.at[s], me)

    def across(s):
        src = kv_ref if s == 0 else all_ref.at[z - s, c, y]
        return remote(src, all_ref.at[z - s, c, y], y_send.at[s], y_recv.at[s], side)

    def between(s):
        pair = all_ref.at[z - s, c]
        return remote(pair, pair, c_send.at[s], c_recv.at[s], sibling)

    for s in range(planes + 1):
        if s < planes:

            @pl.when(z >= s)
            def _(s=s):
                if s > 0:
                    from_below(s).wait_recv()
                if s < planes - 1:

                    @pl.when(z < planes - 1)
                    def _():
                        up(s).start()

                across(s).start()

        if s == 0:
            own.wait()
        else:

            @pl.when(z >= s - 1)
            def _(s=s):
                across(s - 1).wait_recv()
                between(s - 1).start()

    for s in range(planes):

        @pl.when(z >= s)
        def _(s=s):
            if s < planes - 1:

                @pl.when(z < planes - 1)
                def _():
                    up(s).wait_send()

            across(s).wait_send()
            between(s).wait()


def gather_blocks(kv, planes):
    shape = (planes, 2, 2) + kv.shape
    dma = pltpu.SemaphoreType.DMA
    return pl.pallas_call(
        functools.partial(gather_kernel, planes),
        out_shape=jax.ShapeDtypeStruct(shape, kv.dtype),
        in_specs=[pl.BlockSpec(memory_space=pl.ANY)],
        out_specs=pl.BlockSpec(memory_space=pl.ANY),
        scratch_shapes=[dma(())] + [dma((planes,))] * 6,
        compiler_params=pltpu.CompilerParams(collective_id=0, has_side_effects=True),
        name="gather_blocks",
    )(kv)


def attend_kernel(
    chosen_ref, usable_ref, q_ref, do_ref, o_ref, lse_ref, kv_ref,
    dq_ref, part_ref, delta, dq_sum,
):
    slot = pl.program_id(0)
    heads = q_ref.shape[1] // HD

    def columns(h):
        return slice(h * HD, (h + 1) * HD)

    @pl.when(slot == 0)
    def _():
        part_ref[...] = jnp.zeros_like(part_ref)
        dq_sum[...] = jnp.zeros_like(dq_sum)
        for h in range(heads):
            product = do_ref[:, columns(h)].astype(jnp.float32) * o_ref[:, columns(h)].astype(jnp.float32)
            delta[h : h + 1, :] = jnp.sum(product.T, axis=0, keepdims=True)

    def pair(diagonal):
        key = kv_ref[0, 0, 0, :, :HD]
        value = kv_ref[0, 0, 0, :, HD:]
        key_t = key.astype(jnp.float32).T.astype(jnp.bfloat16)
        if diagonal:
            key_pos = lax.broadcasted_iota(jnp.int32, (BLOCK, BLOCK), 0)
            query_pos = lax.broadcasted_iota(jnp.int32, (BLOCK, BLOCK), 1)
            seen = key_pos <= query_pos
        dk = jnp.zeros((BLOCK, HD), jnp.float32)
        dv = jnp.zeros((BLOCK, HD), jnp.float32)
        for h in range(heads):
            query, cotangent = q_ref[:, columns(h)], do_ref[:, columns(h)]
            scores = lax.dot_general(key, query, NT, preferred_element_type=jnp.float32)
            probs = jnp.exp2(scores * (SCALE * LOG2E) - lse_ref[h : h + 1, :] * LOG2E)
            if diagonal:
                probs = jnp.where(seen, probs, 0.0)
            prob_grad = lax.dot_general(value, cotangent, NT, preferred_element_type=jnp.float32)
            score_half = (probs * (prob_grad - delta[h : h + 1, :])).astype(jnp.bfloat16)
            probs_half = probs.astype(jnp.bfloat16)
            dv = dv + lax.dot_general(probs_half, cotangent, NN, preferred_element_type=jnp.float32)
            dk = dk + lax.dot_general(score_half, query, NN, preferred_element_type=jnp.float32)
            dq_sum[h] += lax.dot_general(key_t, score_half, NN, preferred_element_type=jnp.float32)
        block = chosen_ref[slot]
        at = (block // 4, block % 2, (block // 2) % 2)
        part_ref[at + (slice(None), slice(0, HD))] = (dk * SCALE).astype(jnp.bfloat16)
        part_ref[at + (slice(None), slice(HD, 2 * HD))] = dv.astype(jnp.bfloat16)

    @pl.when(slot == 0)
    def _():
        pair(True)

    @pl.when((slot > 0) & (usable_ref[slot] > 0))
    def _():
        pair(False)

    @pl.when(slot == TOPK)
    def _():
        for h in range(heads):
            dq_ref[:, columns(h)] = (dq_sum[h] * SCALE).T.astype(jnp.bfloat16)


def attend(chosen, usable, queries, output_grad, output_rows, lse, blocks):
    rows, width = queries.shape
    heads = width // HD
    whole = lambda s, chosen, usable: (0, 0)
    wide = pl.BlockSpec((rows, width), whole)
    return pl.pallas_call(
        attend_kernel,
        out_shape=(
            jax.ShapeDtypeStruct((rows, width), jnp.bfloat16),
            jax.ShapeDtypeStruct(blocks.shape, jnp.bfloat16),
        ),
        grid_spec=pltpu.PrefetchScalarGridSpec(
            num_scalar_prefetch=2,
            grid=(TOPK + 1,),
            in_specs=[
                wide, wide, wide,
                pl.BlockSpec((heads, rows), whole),
                pl.BlockSpec(
                    (1, 1, 1) + blocks.shape[3:],
                    lambda s, chosen, usable: (
                        chosen[s] // 4, chosen[s] % 2, (chosen[s] // 2) % 2, 0, 0,
                    ),
                ),
            ],
            out_specs=[wide, pl.BlockSpec(blocks.shape, lambda s, chosen, usable: (0,) * 5)],
            scratch_shapes=[
                pltpu.VMEM((heads, rows), jnp.float32),
                pltpu.VMEM((heads, HD, rows), jnp.float32),
            ],
        ),
        compiler_params=pltpu.CompilerParams(vmem_limit_bytes=VMEM_LIMIT),
        cost_estimate=pl.CostEstimate(flops=6 * 10**9, bytes_accessed=10 * 2**20, transcendentals=4 * 2**20),
        name="attend",
    )(chosen, usable, queries, output_grad, output_rows, lse, blocks)


def scatter_kernel(
    planes, part_ref, out_ref, c_in, y_in, z_in, y_out, z_out, held,
    z_send, z_recv, y_send, y_recv, c_send, c_recv,
):
    me, z, y, c = place()
    sibling, side = sibling_of(me, c), beside(me, y)
    greet(sibling)
    greet(side)

    @pl.when(z < planes - 1)
    def _():
        greet(me + 4)

    pl.semaphore_wait(pltpu.get_barrier_semaphore(), 2 + (z > 0).astype(jnp.int32))

    def between(t):
        return remote(part_ref.at[t, 1 - c], c_in.at[t], c_send.at[t], c_recv.at[t], sibling)

    def across(t):
        return remote(y_out.at[t], y_in.at[t], y_send.at[t], y_recv.at[t], side)

    def down(t):
        return remote(z_out.at[t], z_in.at[t], z_send.at[t], z_recv.at[t], me - 4)

    for t in range(planes):

        @pl.when(t <= z)
        def _(t=t):
            between(t).start()

    for t in range(planes):

        @pl.when(t <= z)
        def _(t=t):
            between(t).wait_recv()
            y_out[t] = (
                part_ref[t, c, 1 - y].astype(jnp.float32) + c_in[t, 1 - y].astype(jnp.float32)
            ).astype(jnp.bfloat16)
            across(t).start()
            held[t] = part_ref[t, c, y].astype(jnp.float32) + c_in[t, y].astype(jnp.float32)

    for t in range(planes):

        @pl.when(t <= z)
        def _(t=t):
            across(t).wait_recv()
            held[t] += y_in[t].astype(jnp.float32)

            @pl.when(z < planes - 1)
            def _():
                down(t).wait_recv()
                held[t] += z_in[t].astype(jnp.float32)

            @pl.when(t < z)
            def _():
                z_out[t] = held[t].astype(jnp.bfloat16)
                down(t).start()

            @pl.when(t == z)
            def _():
                out_ref[...] = held[t].astype(jnp.bfloat16)

    for t in range(planes):

        @pl.when(t <= z)
        def _(t=t):
            between(t).wait_send()
            across(t).wait_send()

            @pl.when(t < z)
            def _():
                down(t).wait_send()


def scatter_blocks(part, planes):
    block = part.shape[3:]
    dma = pltpu.SemaphoreType.DMA
    slots = pltpu.VMEM((planes,) + block, jnp.bfloat16)
    return pl.pallas_call(
        functools.partial(scatter_kernel, planes),
        out_shape=jax.ShapeDtypeStruct(block, jnp.bfloat16),
        in_specs=[pl.BlockSpec(memory_space=pltpu.VMEM)],
        out_specs=pl.BlockSpec(memory_space=pltpu.VMEM),
        scratch_shapes=[
            pltpu.VMEM((planes, 2) + block, jnp.bfloat16),
            slots, slots, slots, slots,
            pltpu.VMEM((planes,) + block, jnp.float32),
        ] + [dma((planes,))] * 6,
        compiler_params=pltpu.CompilerParams(
            collective_id=1, has_side_effects=True, vmem_limit_bytes=VMEM_LIMIT
        ),
        cost_estimate=pl.CostEstimate(flops=10**9, bytes_accessed=100 * 2**20, transcendentals=0),
        name="scatter_blocks",
    )(part)


def toward(src, dst, send, recv):
    return pltpu.make_async_remote_copy(
        src_ref=src, dst_ref=dst, send_sem=send, recv_sem=recv,
        device_id={"grp": 1 - lax.axis_index("grp")}, device_id_type=MESH,
    )


def greet_group():
    pl.semaphore_signal(
        pltpu.get_barrier_semaphore(), inc=1,
        device_id={"grp": 1 - lax.axis_index("grp")}, device_id_type=MESH,
    )


def columns(h):
    return slice(h * HD, (h + 1) * HD)


def block_gradients(key, value, q_ref, do_ref, lse_ref, delta_ref, dq_sum, diagonal):
    heads = q_ref.shape[1] // HD
    key_t = key.astype(jnp.float32).T.astype(jnp.bfloat16)
    if diagonal:
        key_pos = lax.broadcasted_iota(jnp.int32, (BLOCK, BLOCK), 0)
        query_pos = lax.broadcasted_iota(jnp.int32, (BLOCK, BLOCK), 1)
        seen = key_pos <= query_pos
    dk = jnp.zeros((BLOCK, HD), jnp.float32)
    dv = jnp.zeros((BLOCK, HD), jnp.float32)
    for h in range(heads):
        query, cotangent = q_ref[:, columns(h)], do_ref[:, columns(h)]
        scores = lax.dot_general(key, query, NT, preferred_element_type=jnp.float32)
        probs = jnp.exp2(scores * (SCALE * LOG2E) - lse_ref[h : h + 1, :] * LOG2E)
        if diagonal:
            probs = jnp.where(seen, probs, 0.0)
        prob_grad = lax.dot_general(value, cotangent, NT, preferred_element_type=jnp.float32)
        score_half = (probs * (prob_grad - delta_ref[h : h + 1, :])).astype(jnp.bfloat16)
        probs_half = probs.astype(jnp.bfloat16)
        dv = dv + lax.dot_general(probs_half, cotangent, NN, preferred_element_type=jnp.float32)
        dk = dk + lax.dot_general(score_half, query, NN, preferred_element_type=jnp.float32)
        dq = lax.dot_general(key_t, score_half, NN, preferred_element_type=jnp.float32)
        dq_sum[h] = dq if diagonal else dq_sum[h] + dq
    return (dk * SCALE).astype(jnp.bfloat16), dv.astype(jnp.bfloat16)


TILE = 256


def fused_kernel(
    planes, selection_ref, key_ref, value_ref, q_ref, do_ref, o_ref, lse_ref, wq_ref, wk_ref, wv_ref,
    out_ref, dkv_far, far_ref,
    blocks, part, delta, dq_sum, picked, dq, dq_far, mine, theirs, total,
    c_in, y_in, z_in, y_out, z_out, held, dkv, summed, extra_in,
    gz_send, gz_recv, gy_send, gy_recv, gc_send, gc_recv,
    sz_send, sz_recv, sy_send, sy_recv, sc_send, sc_recv,
    local_sem, w_send, w_recv, swap_send, swap_recv, x_send, x_recv,
    extra_send, extra_recv, write_sem,
):
    me, z, y, c = place()
    group = lax.axis_index("grp")
    sibling, side = sibling_of(me, c), beside(me, y)
    heads = q_ref.shape[1] // HD
    feature = q_ref.shape[1]
    half = out_ref.shape[1]
    share = half // 2
    kinds = range(2)

    greet(sibling)
    greet(side)
    greet_group()

    @pl.when(z > 0)
    def _():
        greet(me - 4)

    @pl.when(z < planes - 1)
    def _():
        greet(me + 4)

    local_rows = pl.ds(pl.multiple_of(group * half, half), half)
    away_rows = pl.ds(pl.multiple_of((1 - group) * half + c * share, share), share)
    locals_, weights = [], []
    first = 0
    for i, weight in enumerate((wq_ref, wk_ref, wv_ref)):
        last = first + weight.shape[1]
        locals_.append(
            pltpu.make_async_copy(weight.at[local_rows], mine.at[:, first:last], local_sem.at[i])
        )
        weights.append(
            toward(weight.at[away_rows], theirs.at[c, :, first:last], w_send.at[i], w_recv.at[i])
        )
        first = last
    weight_swap = remote(theirs.at[c], theirs.at[c], swap_send, swap_recv, sibling)

    blocks[z, c, 0, y] = key_ref[...]
    blocks[z, c, 1, y] = value_ref[...]
    pl.semaphore_wait(
        pltpu.get_barrier_semaphore(),
        3 + (z > 0).astype(jnp.int32) + (z < planes - 1).astype(jnp.int32),
    )

    def up(s, k):
        slot = blocks.at[z - s, c, k, y]
        return remote(slot, slot, gz_send.at[s, k], gz_recv.at[s + 1, k], me + 4)

    def from_below(s, k):
        slot = blocks.at[z - s, c, k, y]
        return remote(slot, slot, gz_send.at[s, k], gz_recv.at[s, k], me)

    def across(s, k):
        slot = blocks.at[z - s, c, k, y]
        return remote(slot, slot, gy_send.at[s, k], gy_recv.at[s, k], side)

    def between(s, k):
        pair = blocks.at[z - s, c, k]
        return remote(pair, pair, gc_send.at[s, k], gc_recv.at[s, k], sibling)

    def extra_up():
        slot = blocks.at[0, c, 1, 1 - y]
        return remote(slot, slot, extra_send.at[0], extra_recv.at[0], me + 4)

    def gradients(key, value, diagonal):
        return block_gradients(key, value, q_ref, do_ref, lse_ref, delta, dq_sum, diagonal)

    for s in range(planes + 1):
        for k in kinds:
            if s < planes:

                @pl.when(z >= s)
                def _(s=s, k=k):
                    if s > 0:
                        from_below(s, k).wait_recv()
                    if s < planes - 1:

                        @pl.when(z < planes - 1)
                        def _():
                            up(s, k).start()

                    if (s, k) != (planes - 1, 1):
                        across(s, k).start()

            if s > 0:

                @pl.when(z >= s - 1)
                def _(s=s, k=k):
                    if (s, k) != (planes, 1):
                        across(s - 1, k).wait_recv()
                    else:
                        extra_up().wait_recv()
                    if (s, k) == (planes - 1, 1):

                        @pl.when(z == planes - 2)
                        def _():
                            extra_up().start()

                    between(s - 1, k).start()

        if s == 0:
            for copy in weights + locals_:
                copy.start()
            for h in range(heads):
                product = do_ref[:, columns(h)].astype(jnp.float32) * o_ref[:, columns(h)].astype(jnp.float32)
                delta[h : h + 1, :] = jnp.sum(product.T, axis=0, keepdims=True)
            dk, dv = gradients(key_ref[...], value_ref[...], True)
            picked[0, 0] = dk
            picked[0, 1] = dv

        if s == 2:
            for k in kinds:
                between(0, k).wait_recv()

                @pl.when(z >= 1)
                def _(k=k):
                    between(1, k).wait_recv()

            @pl.when(me > 0)
            def _():
                last = me - 1
                dk, dv = gradients(
                    blocks[last // 4, last % 2, 0, (last // 2) % 2],
                    blocks[last // 4, last % 2, 1, (last // 2) % 2],
                    False,
                )
                picked[1, 0] = dk
                picked[1, 1] = dv

    for s in range(2, planes):

        @pl.when(z >= s)
        def _(s=s):
            for k in kinds:
                between(s, k).wait_recv()

    picks = [selection_ref[column, me] for column in range(TOPK)]
    others = [
        jnp.where(picks[0] == me - 1, picks[1], picks[0]),
        jnp.where(picks[2] == me - 1, picks[1], picks[2]),
    ]
    for i, block in enumerate(others):
        usable = block < me
        at = jnp.where(usable, block, me)
        for h in range(heads):
            dq_sum[heads + h] = dq_sum[h]
        dk, dv = gradients(
            blocks[at // 4, at % 2, 0, (at // 2) % 2], blocks[at // 4, at % 2, 1, (at // 2) % 2], False
        )
        for h in range(heads):
            dq_sum[h] = jnp.where(usable, dq_sum[h], dq_sum[heads + h])
        picked[2 + i, 0] = dk
        picked[2 + i, 1] = dv
    for h in range(heads):
        dq[:, columns(h)] = (dq_sum[h] * SCALE).T.astype(jnp.bfloat16)
    query_swap = toward(dq, dq_far, x_send.at[2], x_recv.at[2])
    query_swap.start()

    def inward(t, k):
        return remote(part.at[t, 1 - c, k], c_in.at[t, k], sc_send.at[t, k], sc_recv.at[t, k], sibling)

    def sideways(t, k):
        return remote(y_out.at[t, k], y_in.at[t, k], sy_send.at[t, k], sy_recv.at[t, k], side)

    def down(t, k):
        return remote(z_out.at[t, k], z_in.at[t, k], sz_send.at[t, k], sz_recv.at[t, k], me - 4)

    def extra_down():
        return remote(y_out.at[0, 0], extra_in, extra_send.at[1], extra_recv.at[1], me - 4)

    def keyval_swap(k):
        return toward(dkv.at[k], dkv_far.at[k], x_send.at[k], x_recv.at[k])

    def place_partials(t, core):
        for column in range(2):
            block = t * 4 + column * 2 + core
            for k in kinds:
                nothing = jnp.zeros((BLOCK, HD), jnp.bfloat16)
                chosen = jnp.where((others[0] == block) & (block < me), picked[2, k], nothing)
                chosen = jnp.where((others[1] == block) & (block < me), picked[3, k], chosen)
                part[t, core, k, column] = chosen

                @pl.when(block == me)
                def _(k=k, column=column):
                    part[t, core, k, column] = picked[0, k]

                @pl.when(block == me - 1)
                def _(k=k, column=column):
                    part[t, core, k, column] = picked[1, k]

    for t in range(planes):

        @pl.when(t <= z)
        def _(t=t):
            place_partials(t, 1 - c)
            for k in kinds:
                inward(t, k).start()

    for t in range(planes):

        @pl.when(t <= z)
        def _(t=t):
            place_partials(t, c)
            for k in (1, 0) if t == 0 else (0, 1):
                inward(t, k).wait_recv()
                away = part[t, c, k, 1 - y].astype(jnp.float32) + c_in[t, k, 1 - y].astype(jnp.float32)
                held[t, k] = part[t, c, k, y].astype(jnp.float32) + c_in[t, k, y].astype(jnp.float32)
                if (t, k) != (0, 0):
                    y_out[t, k] = away.astype(jnp.bfloat16)
                    sideways(t, k).start()
                else:

                    @pl.when(z == planes - 1)
                    def _():
                        y_out[t, k] = away.astype(jnp.bfloat16)
                        extra_down().start()
                        z_out[t, k] = held[t, k].astype(jnp.bfloat16)
                        down(t, k).start()

                    @pl.when(z == planes - 2)
                    def _():
                        extra_down().wait_recv()
                        y_out[t, k] = (away + extra_in[...].astype(jnp.float32)).astype(jnp.bfloat16)
                        sideways(t, k).start()

                    @pl.when(z < planes - 2)
                    def _():
                        y_out[t, k] = away.astype(jnp.bfloat16)
                        sideways(t, k).start()

    def dot(lhs, rhs):
        return lax.dot_general(lhs, rhs, NT, preferred_element_type=jnp.float32)

    def tiles(body):
        @pl.loop(0, half // TILE)
        def _(j):
            here = pl.ds(pl.multiple_of(j * TILE, TILE), TILE)
            there = (j * TILE // share, pl.ds(pl.multiple_of(j * TILE % share, TILE), TILE))
            body(here, there)

    for copy in locals_:
        copy.wait()

    def project_query(here, there):
        total[:, here] = dot(dq[...], mine[here, :feature])

    tiles(project_query)
    def project_query_far(here, there):
        total[:, here] += dot(dq_far[...], theirs[there[0], there[1], :feature])

    for t in range(planes):

        @pl.when(t <= z)
        def _(t=t):
            @pl.when(t == jnp.minimum(z, 1))
            def _():
                for copy in weights:
                    copy.wait_recv()
                weight_swap.start()

            @pl.when(t == z)
            def _():
                query_swap.wait()
                weight_swap.wait()
                tiles(project_query_far)

            for k in kinds:

                @pl.when((z < planes - 1) | ((t, k) != (0, 0)))
                def _(k=k):
                    sideways(t, k).wait_recv()
                    held[t, k] += y_in[t, k].astype(jnp.float32)

                @pl.when(z < planes - 1)
                def _(k=k):
                    down(t, k).wait_recv()
                    held[t, k] += z_in[t, k].astype(jnp.float32)

                @pl.when((t < z) & ((z < planes - 1) | ((t, k) != (0, 0))))
                def _(k=k):
                    z_out[t, k] = held[t, k].astype(jnp.bfloat16)
                    down(t, k).start()

                @pl.when(t == z)
                def _(k=k):
                    dkv[k] = held[t, k].astype(jnp.bfloat16)
                    keyval_swap(k).start()

    def project_keyval(here, there):
        summed[:, here] = (
            total[:, here]
            + dot(dkv[0], mine[here, feature : feature + HD])
            + dot(dkv[1], mine[here, feature + HD :])
        ).astype(jnp.bfloat16)

    tiles(project_keyval)
    written = [
        pltpu.make_async_copy(summed, out_ref, write_sem.at[0]),
        pltpu.make_async_copy(theirs.at[:, :, feature:], far_ref, write_sem.at[1]),
    ]
    for copy in written:
        copy.start()
    for s in range(planes):

        @pl.when(z >= s)
        def _(s=s):
            for k in kinds:
                if s < planes - 1:

                    @pl.when(z < planes - 1)
                    def _(k=k):
                        up(s, k).wait_send()

                if (s, k) != (planes - 1, 1):
                    across(s, k).wait_send()
                between(s, k).wait_send()
                inward(s, k).wait_send()

                @pl.when((z < planes - 1) | ((s, k) != (0, 0)))
                def _(k=k):
                    sideways(s, k).wait_send()

                @pl.when(s < z)
                def _(k=k):
                    down(s, k).wait_send()

    @pl.when(z == planes - 2)
    def _():
        extra_up().wait_send()

    @pl.when(z == planes - 1)
    def _():
        extra_down().wait_send()

    for copy in weights:
        copy.wait_send()
    for k in kinds:
        keyval_swap(k).wait()
    for copy in written:
        copy.wait()


def finish_kernel(summed_ref, dkv_ref, far_ref, out_ref):
    out_ref[...] = (
        summed_ref[...].astype(jnp.float32)
        + lax.dot_general(dkv_ref[0], far_ref[:, :HD], NT, preferred_element_type=jnp.float32)
        + lax.dot_general(dkv_ref[1], far_ref[:, HD:], NT, preferred_element_type=jnp.float32)
    ).astype(jnp.bfloat16)


def finish(summed, dkv_far, far):
    rows, half = summed.shape
    wide = 2 * TILE
    column = pl.BlockSpec((rows, wide), lambda j: (0, j))
    return pl.pallas_call(
        finish_kernel,
        out_shape=jax.ShapeDtypeStruct(summed.shape, jnp.bfloat16),
        grid=(half // wide,),
        in_specs=[
            column,
            pl.BlockSpec(dkv_far.shape, lambda j: (0, 0, 0)),
            pl.BlockSpec((wide, far.shape[1]), lambda j: (j, 0)),
        ],
        out_specs=column,
        name="finish",
    )(summed, dkv_far, far)


def fused(selection, key, value, queries, output_grad, output_rows, lse, weights, planes):
    rows, width = queries.shape
    heads = width // HD
    half = weights[0].shape[0] // 2
    features = sum(weight.shape[1] for weight in weights)
    dma = pltpu.SemaphoreType.DMA
    vmem = pl.BlockSpec(memory_space=pltpu.VMEM)
    anywhere = pl.BlockSpec(memory_space=pl.ANY)

    def half_type(*shape):
        return pltpu.VMEM(shape, jnp.bfloat16)

    def full_type(*shape):
        return pltpu.VMEM(shape, jnp.float32)

    slots = half_type(planes, 2, rows, HD)
    summed, dkv_far, far = pl.pallas_call(
        functools.partial(fused_kernel, planes),
        out_shape=(
            jax.ShapeDtypeStruct((rows, half), jnp.bfloat16),
            jax.ShapeDtypeStruct((2, rows, HD), jnp.bfloat16),
            jax.ShapeDtypeStruct((2, half // 2, 2 * HD), jnp.bfloat16),
        ),
        in_specs=[pl.BlockSpec(memory_space=pltpu.SMEM)] + [vmem] * 6 + [anywhere] * 3,
        out_specs=(anywhere,) * 3,
        scratch_shapes=[
            half_type(planes, 2, 2, 2, rows, HD),
            half_type(planes, 2, 2, 2, rows, HD),
            full_type(heads, rows),
            full_type(2 * heads, HD, rows),
            half_type(4, 2, rows, HD),
            half_type(rows, width),
            half_type(rows, width),
            half_type(half, features),
            half_type(2, half // 2, features),
            full_type(rows, half),
            half_type(planes, 2, 2, rows, HD),
            slots, slots, slots, slots,
            full_type(planes, 2, rows, HD),
            half_type(2, rows, HD),
            half_type(rows, half),
            half_type(rows, HD),
        ] + [dma((planes, 2))] * 12 + [dma((3,)), dma((3,)), dma((3,)), dma(()), dma(()), dma((3,)), dma((3,)), dma((2,)), dma((2,)), dma((2,))],
        compiler_params=pltpu.CompilerParams(
            collective_id=2, has_side_effects=True, vmem_limit_bytes=VMEM_LIMIT
        ),
        name="fused",
    )(selection, key, value, queries, output_grad, output_rows, lse, *weights)
    return finish(summed, dkv_far, far.reshape(half, 2 * HD))


def on_device(
    queries, key_rows, value_rows, output_rows, output_grad, log_normalizer,
    selection, query_weight, key_weight, value_weight,
):
    position = lax.axis_index("ctx")
    contexts = lax.axis_size("ctx")
    groups = lax.axis_size("grp")
    planes = contexts // 4
    if groups == 2:
        weights = (query_weight, key_weight, value_weight)
        lse = log_normalizer.T
        return fused(
            selection.T, key_rows, value_rows, queries, output_grad, output_rows, lse, weights, planes
        )

    blocks = gather_blocks(jnp.concatenate([key_rows, value_rows], axis=1), planes)
    row = lax.dynamic_index_in_dim(selection, position, 0, keepdims=False).astype(jnp.int32)
    chosen = jnp.concatenate([position[None].astype(jnp.int32), row])
    usable = jnp.concatenate([jnp.ones((1,), jnp.int32), (row < position).astype(jnp.int32)])
    grad_query, part = attend(
        chosen, usable, queries, output_grad, output_rows, log_normalizer.T, blocks
    )
    grad_keyval = scatter_blocks(part, planes)
    dot = functools.partial(lax.dot_general, dimension_numbers=NT, preferred_element_type=jnp.float32)
    combined = dot(grad_query, query_weight)
    combined = combined + dot(grad_keyval[:, :HD], key_weight)
    combined = combined + dot(grad_keyval[:, HD:], value_weight)
    return lax.psum_scatter(combined.astype(jnp.bfloat16), "grp", scatter_dimension=1, tiled=True)


def solution(mesh):
    return jax.shard_map(
        on_device,
        mesh=mesh,
        in_specs=(
            P("ctx", "grp"),
            P("ctx", "grp"),
            P("ctx", "grp"),
            P("ctx", "grp"),
            P("ctx", "grp"),
            P("ctx", "grp"),
            P(),
            P(None, "grp"),
            P(None, "grp"),
            P(None, "grp"),
        ),
        out_specs=P("ctx", "grp"),
        check_vma=False,
    )
```
